256 devices in a mesh: dp: 2 (over y_hi), fsdp: 8 (over x, y_lo), expert: 16 (over z, core).
Axes of the slice: x: 4, y: 4 (y_hi: 2, y_lo: 2; y = y_hi * 2 + y_lo), z: 8, core: 2. Of those that a mesh axis runs over, the one named last changes fastest.
Arguments:
- tokens: bfloat16 [65536, 2048], P(('dp', 'fsdp', 'expert')), may hold values from -6 to 6
- expert_ids: int32 [65536, 8], P(('dp', 'fsdp', 'expert')), may hold values from 0 to 127, all different within a row; in each aligned block of 256 rows (0 to 255, 256 to 511, ...) at most 24 rows name the same one
- gate_units: int32 [65536, 8], P(('dp', 'fsdp', 'expert')), may hold values from 1 to 256
- expert_weights: bfloat16 [16, 2048, 3, 768], P('expert', ('dp', 'fsdp')), may hold values from -0.125 to 0.125
- out_grad: bfloat16 [65536, 2048], P(('dp', 'fsdp', 'expert')), may hold values from -6 to 6
Outputs:
- moe_out: bfloat16 [65536, 2048], P(('dp', 'fsdp', 'expert'))
- token_grad: bfloat16 [65536, 2048], P(('dp', 'fsdp', 'expert'))
- weight_grad: bfloat16 [16, 2048, 3, 768], P('expert', ('dp', 'fsdp'))
The draws below stay inside these ranges and needn't reach their ends.
Inputs may be any that keep to these rules, and one draw needn't show every extreme that they name: `expert_ids`: each row names 8 different experts; the 256 rows of one device name one expert at most 24 times.
All inputs are finite; a program needn't handle non-finite values.
Results may differ from the reference program's by a relative error of at most 0.018.
Values may be sent and summed in bfloat16 or wider, within the bound.
A program may use at most 128 MiB of HBM per device.

```python
import math
import jax
import jax.numpy as jnp
import numpy as np
from jax import lax

D = 2048
H = 768
ROUTED = 128
TOPK = 8
TOK_DEV = 256
CAP = 24
EXPERTS = 16
TOKENS = 65536
N_DP = 2
N_FSDP = 8
N_EXPERT = 16


def place_ends(array, key, least, high):
    longest = array.shape.index(max(array.shape))
    spots = []
    for shift in (0, 1):
        where = [jax.random.randint(jax.random.fold_in(key, axis), (), 0, length) for axis, length in enumerate(array.shape)]
        where[longest] = (where[longest] + shift) % array.shape[longest]
        spots.append(tuple(where))
    return array.at[spots[0]].set(least).at[spots[1]].set(high)


def shard_levels(key, extent, pieces, least, high):
    loudness, own = 1.0, jax.random.fold_in(key, 6)
    for dim, parts in pieces:
        draws = jnp.exp(jax.random.uniform(jax.random.fold_in(own, dim), (parts,), jnp.float32, least / len(pieces), high / len(pieces)))
        loudness = loudness * jnp.repeat(draws, extent[dim] // parts).reshape([-1 if axis == dim else 1 for axis in range(len(extent))])
    return loudness


def shared_out(own_key, own, number, rows, amount, top, bound, lean):
    sequence = jax.random.permutation(own_key, amount)
    crowded, ordinary = load_shares(amount, rows * top, bound, lean, True), load_shares(amount, rows * top, bound, lean, False)
    places = jnp.arange(amount)

    def named(sizes, offset_by):
        used = int((sizes > 0).sum())
        fixed = max(1, used // 4)
        shifted = fixed + (places - fixed + offset_by * (used - fixed)) % max(1, amount - fixed)
        return jnp.zeros((amount,), jnp.int32).at[sequence[jnp.where(places < fixed, places, shifted)]].set(jnp.asarray(sizes, jnp.int32))

    sizes = jnp.where(number % 4 == 0, named(crowded, number // 4), named(ordinary, number - number // 4 - 1))
    mixed = jax.random.permutation(jax.random.fold_in(own, 3), amount)
    donor, sink = mixed[0:amount // 2 * 2:2], mixed[1:amount // 2 * 2:2]
    margin = jnp.minimum(sizes[donor] - 1, bound - sizes[sink]) // 2
    margin = jnp.where((donor == sequence[0]) | (sink == sequence[0]) | (sizes[sink] == 0), 0, jnp.maximum(margin, 0))
    shifted = jax.random.randint(jax.random.fold_in(own, 4), (amount // 2,), 0, 1 << 20) % (margin + 1)
    sizes = sizes.at[donor].add(-shifted).at[sink].add(shifted)
    items = jnp.searchsorted(jnp.cumsum(sizes), jnp.arange(rows * top), side="right").astype(jnp.int32)
    listing = items.reshape(top, rows).T
    listing = listing[jax.random.permutation(jax.random.fold_in(own, 1), rows)]
    offset_by = jax.random.randint(jax.random.fold_in(own, 2), (rows, 1), 0, top)
    return jnp.take_along_axis(listing, (jnp.arange(top)[None, :] + offset_by) % top, axis=1)


def load_shares(count, total, most, lean, full):
    loads = [(1 << 20) // math.isqrt(rank ** lean) + 1 for rank in range(1, count + 1)]
    largest = most if full else min(most, max(-(-total // count), total * loads[0] // sum(loads)))
    least = 1 if total - largest >= count - 1 else 0
    holding, rest = [largest] + [least] * (count - 1), total - largest - least * (count - 1)
    while rest > 0:
        candidates = [i for i in range(1, count) if holding[i] < largest] or [i for i in range(1, count) if holding[i] < most]
        mass, left = sum([loads[i] for i in candidates]), rest
        for i in candidates:
            addition = min(most - holding[i], max(1, left * loads[i] // mass), rest)
            holding[i] = holding[i] + addition
            rest = rest - addition
    return np.array(holding)


def bell_draw(own_key, extent, deviation, reach, shards=(), kind=jnp.bfloat16):
    values = deviation * jax.random.normal(own_key, extent, jnp.float32)
    if shards:
        values = values * shard_levels(own_key, extent, shards, -0.22, 0.18)
    return jnp.clip(values, -reach, reach).astype(kind)


def setup_inputs(seed: int = 0) -> dict:
    key_list = jax.random.split(jax.random.key(seed), 6)
    tokens = bell_draw(key_list[0], (TOKENS, D), 1.0, 6.0, ((0, 256),))
    expert_ids_keys = jax.random.split(jax.random.fold_in(key_list[1], 1), TOKENS // TOK_DEV)
    expert_ids_turns = jax.random.permutation(jax.random.fold_in(key_list[1], 3), TOKENS // TOK_DEV)
    expert_ids = jax.vmap(lambda own, number: shared_out(jax.random.fold_in(key_list[1], 2), own, number, TOK_DEV, ROUTED, TOPK, CAP, 0))(expert_ids_keys, expert_ids_turns).reshape((TOKENS, TOPK))
    gate_units = place_ends(jax.random.randint(key_list[2], (TOKENS, TOPK), 1, 257), jax.random.fold_in(key_list[2], 1), 1, 256).astype(jnp.int32)
    expert_weights = bell_draw(key_list[3], (EXPERTS, D, 3, H), D ** -0.5, 0.125, ((0, 16), (1, 16)))
    out_grad = bell_draw(key_list[4], (TOKENS, D), 1.0, 6.0, ((0, 256),))
    return dict(tokens=tokens, expert_ids=expert_ids, gate_units=gate_units, expert_weights=expert_weights, out_grad=out_grad)


def slot_tables(expert_ids, gate_units):
    blocks = N_DP * N_FSDP * N_EXPERT
    token_total = expert_ids.shape[0]
    top_count = expert_ids.shape[1]
    per_block = token_total // blocks
    block_ids = expert_ids.reshape(blocks, per_block * top_count)
    chosen = (block_ids[:, :, None] == jnp.arange(N_EXPERT, dtype=jnp.int32)[None, None, :]).astype(jnp.int32)
    before = jnp.cumsum(chosen, axis=1) - chosen
    ranking = jnp.sum(before * chosen, axis=2).astype(jnp.int32)
    block_index = jnp.arange(blocks, dtype=jnp.int32)[:, None]
    group_index = block_index // N_EXPERT
    source = block_index % N_EXPERT
    per_expert = blocks * CAP
    position = group_index * (N_EXPERT * CAP) + source * CAP + ranking
    inside = block_ids < N_EXPERT
    flat_index = jnp.where(inside, block_ids * per_expert + position, N_EXPERT * per_expert).reshape(-1).astype(jnp.int32)
    token_index = jnp.repeat(jnp.arange(token_total, dtype=jnp.int32), top_count)
    gate_values = gate_units.reshape(-1).astype(jnp.float32) / 256.0
    token_table = jnp.full((N_EXPERT * per_expert,), token_total, jnp.int32).at[flat_index].set(token_index, mode="drop")
    gate_table = jnp.zeros((N_EXPERT * per_expert,), jnp.float32).at[flat_index].set(gate_values, mode="drop")
    return token_table.reshape(N_EXPERT, per_expert), gate_table.reshape(N_EXPERT, per_expert)


def expert_pass(token_table, gate_table, expert_weight, padded_tokens, padded_grad):
    model_width = padded_tokens.shape[1]
    hidden_units = expert_weight.shape[2]
    flat_weights = expert_weight.reshape(model_width, 3 * hidden_units)
    slot_rows = padded_tokens[token_table]
    grad_rows = padded_grad[token_table]
    gate_up = jnp.dot(slot_rows, flat_weights[:, :2 * hidden_units], preferred_element_type=jnp.float32)
    gate_act = gate_up[:, :hidden_units]
    up_act = gate_up[:, hidden_units:]
    sigmoid_gate = jax.nn.sigmoid(gate_act)
    swish_gate = gate_act * sigmoid_gate
    activation = (swish_gate * up_act).astype(jnp.bfloat16)
    down_rows = flat_weights[:, 2 * hidden_units:]
    result = lax.dot_general(activation, down_rows, (((1,), (1,)), ((), ())), preferred_element_type=jnp.float32).astype(jnp.bfloat16)
    scaled = (gate_table[:, None] * grad_rows.astype(jnp.float32)).astype(jnp.bfloat16)
    hidden_grad = jnp.dot(scaled, down_rows, preferred_element_type=jnp.float32)
    gate_grad = (hidden_grad * up_act * sigmoid_gate * (1.0 + gate_act * (1.0 - sigmoid_gate))).astype(jnp.bfloat16)
    up_grad = (hidden_grad * swish_gate).astype(jnp.bfloat16)
    pair_grad = jnp.concatenate([gate_grad, up_grad], axis=1)
    row_grad = lax.dot_general(pair_grad, flat_weights[:, :2 * hidden_units], (((1,), (1,)), ((), ())), preferred_element_type=jnp.float32).astype(jnp.bfloat16)
    groups = N_DP * N_FSDP
    per_group = slot_rows.shape[0] // groups
    grouped_rows = slot_rows.reshape(groups, per_group, model_width).astype(jnp.float32)
    grouped_pair = pair_grad.reshape(groups, per_group, 2 * hidden_units).astype(jnp.float32)
    grouped_scaled = scaled.reshape(groups, per_group, model_width).astype(jnp.float32)
    grouped_act = activation.reshape(groups, per_group, hidden_units).astype(jnp.float32)
    input_term = jnp.einsum("gsd,gsh->gdh", grouped_rows, grouped_pair, precision=lax.Precision.HIGHEST)
    down_term = jnp.einsum("gsd,gsh->gdh", grouped_scaled, grouped_act, precision=lax.Precision.HIGHEST)
    group_terms = jnp.concatenate([input_term, down_term], axis=2).astype(jnp.bfloat16)
    group_terms = lax.optimization_barrier(group_terms).astype(jnp.float32)
    summed = jnp.sum(group_terms, axis=0).reshape(model_width, 3, hidden_units).astype(jnp.bfloat16)
    return result, row_grad, summed


def reference(tokens, expert_ids, gate_units, expert_weights, out_grad):
    token_table, gate_table = slot_tables(expert_ids, gate_units)
    token_total = tokens.shape[0]
    model_width = tokens.shape[1]
    padded_tokens = jnp.concatenate([tokens, jnp.zeros((1, model_width), jnp.bfloat16)], axis=0)
    padded_grad = jnp.concatenate([out_grad, jnp.zeros((1, model_width), jnp.bfloat16)], axis=0)

    def expert_step(packed):
        return expert_pass(packed[0], packed[1], packed[2], padded_tokens, padded_grad)

    results, row_grads, weight_grad = lax.map(expert_step, (token_table, gate_table, expert_weights))
    flat_table = token_table.reshape(-1)
    outputs = jnp.zeros((token_total + 1, model_width), jnp.float32).at[flat_table].add(
        gate_table.reshape(-1)[:, None] * results.reshape(-1, model_width).astype(jnp.float32))
    grads = jnp.zeros((token_total + 1, model_width), jnp.float32).at[flat_table].add(
        row_grads.reshape(-1, model_width).astype(jnp.float32))
    return outputs[:token_total].astype(jnp.bfloat16), grads[:token_total].astype(jnp.bfloat16), weight_grad
```

```python
import functools

import jax
import jax.numpy as jnp
from jax import lax
from jax.experimental import pallas as pl
from jax.experimental.pallas import tpu as pltpu
from jax.sharding import PartitionSpec as P

CAP = 24
SLOTS = 16
ROWS = CAP * SLOTS
MESH = pl.DeviceIdType.MESH
BF16 = jnp.bfloat16
F32 = jnp.float32

OFFSETS = [(dz, dc) for dz in (0, 1, 7, 2, 6, 3, 5, 4) for dc in (0, 1)]
CHUNKS = ((0, 10), (10, 14), (14, 16))
PIECES = ((0, 6), (6, 10), (10, 14), (14, 16))


def place():
    dp, fsdp, expert = (lax.axis_index(n) for n in ("dp", "fsdp", "expert"))
    return lax.div(fsdp, 2), dp * 2 + lax.rem(fsdp, 2), lax.div(expert, 2), lax.rem(expert, 2)


def device(x, y, z, core):
    return (lax.div(y, 2), x * 2 + lax.rem(y, 2), z * 2 + core)


def kernel(
    tokens, ids, units, weights, out_grad,
    moe_out, token_grad, weight_grad,
    full, term, reduced, row_send, grad_send, row_recv, grad_recv,
    res_send, back_send, res_recv, back_recv, rows, grads, act, gate_grad, up_grad,
    pick, weigh,
    out_s, out_r, ret_s, ret_r, ag_s, ag_r, rs_s, rs_r,
):
    x, y, z, core = place()
    width = tokens.shape[1]
    hidden = weights.shape[2]

    def peer(slot, sign):
        dz, dc = OFFSETS[slot]
        return device(x, y, lax.rem(z + (sign * dz) % 8, 8), lax.rem(core + dc, 2))

    def near(axis, step):
        if axis == 0:
            return device(lax.rem(x + step % 4, 4), y, z, core)
        return device(x, lax.rem(y + step % 4, 4), z, core)

    def block(half, first, second):
        dx, dy = (first, second) if half == 0 else (second, first)
        bx, by = lax.rem(x + dx % 4, 4), lax.rem(y + dy % 4, 4)
        return lax.div(by, 2) * 8 + bx * 2 + lax.rem(by, 2)

    barrier = pltpu.get_barrier_semaphore()
    for slot in range(1, SLOTS):
        pl.semaphore_signal(barrier, inc=1, device_id=peer(slot, 1), device_id_type=MESH)
    for axis in (0, 1):
        for step in (1, -1):
            pl.semaphore_signal(barrier, inc=1, device_id=near(axis, step), device_id_type=MESH)

    mine = block(0, 0, 0)
    full[mine] = weights[...]
    pl.semaphore_wait(barrier, SLOTS - 1 + 4)

    sent = []

    def send(src, dst, send_sem, recv_sem, to):
        copy = pltpu.make_async_remote_copy(
            src_ref=src, dst_ref=dst, send_sem=send_sem, recv_sem=recv_sem,
            device_id=to, device_id_type=MESH,
        )
        copy.start()
        sent.append(copy)
        return copy

    ag = {}

    def part(which, half):
        base = 64 * half
        return {"w": pl.ds(base, 64), "p": pl.ds(base, 32), "q": pl.ds(base + 32, 32)}[which]

    def gather_send(half, index, at, which, axis, step):
        ref = full.at[at, :, part(which, half), :]
        ag[half, index] = send(ref, ref, ag_s.at[half, index], ag_r.at[half, index], near(axis, step))

    ITEMS = (0, -1, 1, 2)

    def gather_own(half):
        a1, a2 = (0, 1) if half == 0 else (1, 0)
        gather_send(half, 0, mine, "w", a1, 1)
        gather_send(half, 1, mine, "w", a1, -1)

    def gather_item(half, k):
        a2 = 1 if half == 0 else 0
        at = block(half, ITEMS[k], 0)
        gather_send(half, 4 + 4 * k, at, "w", a2, 1)
        gather_send(half, 5 + 4 * k, at, "w", a2, -1)

    def gather_forward_first(half):
        a1 = 0 if half == 0 else 1
        ag[half, 0].wait_recv()
        gather_send(half, 2, block(half, -1, 0), "p", a1, 1)
        ag[half, 1].wait_recv()
        gather_send(half, 3, block(half, 1, 0), "q", a1, -1)

    def gather_forward_item(half, k):
        a2 = 1 if half == 0 else 0
        ag[half, 4 + 4 * k].wait_recv()
        gather_send(half, 6 + 4 * k, block(half, ITEMS[k], -1), "p", a2, 1)
        ag[half, 5 + 4 * k].wait_recv()
        gather_send(half, 7 + 4 * k, block(half, ITEMS[k], 1), "q", a2, -1)

    for half in (0, 1):
        gather_own(half)
    for half in (0, 1):
        gather_item(half, 0)

    lane = lax.broadcasted_iota(jnp.int32, (1, ROWS), 1)
    slot_of = jnp.zeros((1, ROWS), jnp.int32)
    for j in range(1, SLOTS):
        slot_of = slot_of + (lane >= CAP * j).astype(jnp.int32)
    rank_of = (lane - slot_of * CAP).astype(F32)
    pair = slot_of >> 1
    dz = jnp.where((pair & 1) == 1, (pair + 1) >> 1, (8 - (pair >> 1)) & 7)
    named = ((z + dz) & 7) * 2 + ((core + (slot_of & 1)) & 1)
    token_count = tokens.shape[0]
    chosen = jnp.zeros((token_count, ROWS), F32)
    id_table = ids[...]
    unit_table = units[...].astype(F32)
    for k in range(ids.shape[1]):
        chosen = chosen + jnp.where(id_table[:, k : k + 1] == named, unit_table[:, k : k + 1], 0.0)
    earlier = (
        lax.broadcasted_iota(jnp.int32, (token_count, token_count), 1)
        < lax.broadcasted_iota(jnp.int32, (token_count, token_count), 0)
    ).astype(F32).astype(BF16)
    ranking = jnp.dot(
        earlier, (chosen > 0.0).astype(F32).astype(BF16), preferred_element_type=F32
    )
    gate = jnp.where(ranking == rank_of, chosen, 0.0)
    weigh[...] = (jnp.transpose(gate) * (1.0 / 256.0)).astype(BF16)
    pick[...] = jnp.transpose((gate > 0.0).astype(F32)).astype(BF16)

    out = {}

    def dispatch(lo, hi):
        cols = 512

        def tile(i, _):
            at = pl.ds(pl.multiple_of(i * cols, cols), cols)
            for table, source, to in ((pick, tokens, row_send), (weigh, out_grad, grad_send)):
                got = jnp.dot(
                    table[CAP * lo : CAP * hi, :], source[:, at], preferred_element_type=F32
                )
                to[lo:hi, :, at] = got.reshape(hi - lo, CAP, cols).astype(BF16)
            return 0

        lax.fori_loop(0, width // cols, tile, 0)
        for slot in range(max(lo, 1), hi):
            for a, (src, dst) in enumerate(((row_send, row_recv), (grad_send, grad_recv))):
                out[a, slot] = send(
                    src.at[slot], dst.at[slot], out_s.at[a, slot], out_r.at[a, slot], peer(slot, 1)
                )

    dispatch(*PIECES[0])
    row_recv[0] = row_send[0]
    grad_recv[0] = grad_send[0]
    dispatch(*PIECES[1])
    for half in (0, 1):
        gather_forward_first(half)
    for half in (0, 1):
        gather_item(half, 1)
        gather_item(half, 2)
    dispatch(*PIECES[2])
    dispatch(*PIECES[3])
    for half in (0, 1):
        gather_forward_item(half, 0)
    for half in (0, 1):
        ag[half, 2].wait_recv()
        ag[half, 3].wait_recv()
        gather_item(half, 3)
    for k in (1, 2, 3):
        for half in (0, 1):
            gather_forward_item(half, k)
    for k in range(4):
        for half in (0, 1):
            ag[half, 6 + 4 * k].wait_recv()
            ag[half, 7 + 4 * k].wait_recv()

    ret = {}
    nt = (((1,), (1,)), ((), ()))
    tn = (((0,), (0,)), ((), ()))

    def experts(lo, hi):
        r0, r1 = CAP * lo, CAP * hi
        for slot in range(max(lo, 1), hi):
            for a in (0, 1):
                out[a, slot].wait_recv()

        def pack(i, _):
            at = pl.ds(pl.multiple_of(i * 512, 512), 512)
            for src, dst in ((row_recv, rows), (grad_recv, grads)):
                dst[r0:r1, at] = src[lo:hi, :, at].astype(F32).reshape(r1 - r0, 512).astype(BF16)
            return 0

        lax.fori_loop(0, width // 512, pack, 0)

        def inner(i, _):
            at = pl.ds(pl.multiple_of(i * 256, 256), 256)
            w = [full[:, j, :, at].reshape(width, 256) for j in range(3)]
            g = jnp.dot(rows[r0:r1, :], w[0], preferred_element_type=F32)
            u = jnp.dot(rows[r0:r1, :], w[1], preferred_element_type=F32)
            hg = jnp.dot(grads[r0:r1, :], w[2], preferred_element_type=F32)
            s = jax.nn.sigmoid(g)
            swish = g * s
            act[r0:r1, at] = (swish * u).astype(BF16)
            gate_grad[r0:r1, at] = (hg * u * s * (1.0 + g * (1.0 - s))).astype(BF16)
            up_grad[r0:r1, at] = (hg * swish).astype(BF16)
            return 0

        lax.fori_loop(0, hidden // 256, inner, 0)

        def outer(i, _):
            at = pl.ds(pl.multiple_of(i * 256, 256), 256)
            w = [full[pl.ds(2 * i, 2), j].reshape(256, hidden) for j in range(3)]
            res = lax.dot_general(act[r0:r1, :], w[2], nt, preferred_element_type=F32)
            res_send[lo:hi, :, at] = res.reshape(hi - lo, CAP, 256).astype(BF16)
            back = lax.dot_general(gate_grad[r0:r1, :], w[0], nt, preferred_element_type=F32)
            back = back + lax.dot_general(up_grad[r0:r1, :], w[1], nt, preferred_element_type=F32)
            back_send[lo:hi, :, at] = back.reshape(hi - lo, CAP, 256).astype(BF16)
            return 0

        lax.fori_loop(0, width // 256, outer, 0)
        for slot in range(max(lo, 1), hi):
            for a, (src, dst) in enumerate(((res_send, res_recv), (back_send, back_recv))):
                ret[a, slot] = send(
                    src.at[slot], dst.at[slot], ret_s.at[a, slot], ret_r.at[a, slot], peer(slot, -1)
                )
        if lo == 0:
            res_recv[0] = res_send[0]
            back_recv[0] = back_send[0]

    for lo, hi in CHUNKS:
        experts(lo, hi)

    def terms(i, _):
        at = pl.ds(pl.multiple_of(i * 256, 256), 256)
        for j, (left, right) in enumerate(((rows, gate_grad), (rows, up_grad), (grads, act))):
            got = lax.dot_general(left[:, at], right[...], tn, preferred_element_type=F32)
            term[pl.ds(2 * i, 2), j] = got.reshape(2, 128, hidden).astype(BF16)
        return 0

    lax.fori_loop(0, width // 256, terms, 0)

    rs = {}

    def reduce_send(half, index, at, which, axis, step):
        rs[half, index] = send(
            term.at[at, :, part(which, half), :], reduced.at[half, index],
            rs_s.at[half, index], rs_r.at[half, index], near(axis, step),
        )

    def add_into(half, at, which, indices):
        rows_at = part(which, half)
        for j in range(3):
            total = term[at, j, rows_at, :].astype(F32)
            for index in indices:
                total = total + reduced[half, index, j].astype(F32)
            term[at, j, rows_at, :] = total.astype(BF16)

    def ring(half, base, axis, at):
        def start():
            reduce_send(half, base + 0, at(2), "q", axis, 1)
            reduce_send(half, base + 1, at(2), "p", axis, -1)
            reduce_send(half, base + 2, at(1), "p", axis, 1)
            reduce_send(half, base + 3, at(-1), "q", axis, -1)

        def forward():
            rs[half, base + 0].wait_recv()
            add_into(half, at(1), "q", (base + 0,))
            reduce_send(half, base + 4, at(1), "q", axis, 1)
            rs[half, base + 1].wait_recv()
            add_into(half, at(-1), "p", (base + 1,))
            reduce_send(half, base + 5, at(-1), "p", axis, -1)

        def finish():
            for index in (2, 5):
                rs[half, base + index].wait_recv()
            add_into(half, at(0), "p", (base + 2, base + 5))
            for index in (3, 4):
                rs[half, base + index].wait_recv()
            add_into(half, at(0), "q", (base + 3, base + 4))

        return start, forward, finish

    first = {}
    ORDER = (2, 1, -1, 0)
    for k, i in enumerate(ORDER):
        for half in (0, 1):
            first[half, k] = ring(
                half, 6 * k, 1 if half == 0 else 0, functools.partial(block, half, i)
            )
    second = {
        half: ring(half, 24, 0 if half == 0 else 1, lambda j, half=half: block(half, j, 0))
        for half in (0, 1)
    }
    for stage in (0, 1):
        for k in range(4):
            for half in (0, 1):
                first[half, k][stage]()
    for k in range(4):
        for half in (0, 1):
            first[half, k][2]()
    for stage in (0, 1, 2):
        for half in (0, 1):
            second[half][stage]()
    weight_grad[...] = term[mine]

    for slot in range(1, SLOTS):
        for a in (0, 1):
            ret[a, slot].wait_recv()

    def combine(i, _):
        at = pl.ds(pl.multiple_of(i * 256, 256), 256)
        for table, source, to in ((weigh, res_recv, moe_out), (pick, back_recv, token_grad)):
            got = source[:, :, at].astype(F32).reshape(ROWS, 256).astype(BF16)
            to[:, at] = lax.dot_general(table[...], got, tn, preferred_element_type=F32).astype(BF16)
        return 0

    lax.fori_loop(0, width // 256, combine, 0)
    for copy in sent:
        copy.wait_send()


def on_device(tokens, expert_ids, gate_units, expert_weights, out_grad):
    count, width = tokens.shape
    _, part, kinds, hidden = expert_weights.shape
    blocks = width // part
    vmem = pl.BlockSpec(memory_space=pltpu.VMEM)
    slots = pltpu.VMEM((SLOTS, CAP, width), BF16)
    sem = pltpu.SemaphoreType.DMA
    moe_out, token_grad, weight_grad = pl.pallas_call(
        kernel,
        out_shape=(
            jax.ShapeDtypeStruct((count, width), BF16),
            jax.ShapeDtypeStruct((count, width), BF16),
            jax.ShapeDtypeStruct((kinds, part, hidden), BF16),
        ),
        in_specs=[vmem] * 5,
        out_specs=(vmem, vmem, vmem),
        scratch_shapes=[
            pltpu.VMEM((blocks, kinds, part, hidden), BF16),
            pltpu.VMEM((blocks, kinds, part, hidden), BF16),
            pltpu.VMEM((2, 30, kinds, part // 4, hidden), BF16),
            *([slots] * 8),
            *([pltpu.VMEM((ROWS, width), BF16)] * 2),
            *([pltpu.VMEM((ROWS, hidden), BF16)] * 3),
            *([pltpu.VMEM((ROWS, count), BF16)] * 2),
            sem((2, SLOTS)), sem((2, SLOTS)), sem((2, SLOTS)), sem((2, SLOTS)),
            sem((2, 20)), sem((2, 20)), sem((2, 30)), sem((2, 30)),
        ],
        compiler_params=pltpu.CompilerParams(
            collective_id=0, has_side_effects=True, vmem_limit_bytes=62 * 1024 * 1024
        ),
        name="experts",
    )(tokens, expert_ids, gate_units, jnp.transpose(expert_weights[0], (1, 0, 2)), out_grad)
    return moe_out, token_grad, jnp.transpose(weight_grad, (1, 0, 2))[None]


def solution(mesh):
    rows = P(("dp", "fsdp", "expert"), None)
    split = P("expert", ("dp", "fsdp"), None, None)
    return jax.shard_map(
        on_device,
        mesh=mesh,
        in_specs=(rows, rows, rows, split, rows),
        out_specs=(rows, rows, split),
        check_vma=False,
    )
```

```python
import functools

import jax
import jax.numpy as jnp
from jax import lax
from jax.experimental import pallas as pl
from jax.experimental.pallas import tpu as pltpu
from jax.sharding import PartitionSpec as P

CAP = 24
SLOTS = 16
ROWS = CAP * SLOTS
MESH = pl.DeviceIdType.MESH
BF16 = jnp.bfloat16
F32 = jnp.float32

OFFSETS = [(dz, dc) for dz in (0, 1, 7, 2, 6, 3, 5, 4) for dc in (0, 1)]
CHUNKS = ((0, 10), (10, 14), (14, 16))
PIECES = ((2, 6), (6, 10), (10, 14), (14, 16), (0, 2))


def place():
    dp, fsdp, expert = (lax.axis_index(n) for n in ("dp", "fsdp", "expert"))
    return lax.div(fsdp, 2), dp * 2 + lax.rem(fsdp, 2), lax.div(expert, 2), lax.rem(expert, 2)


def device(x, y, z, core):
    return (lax.div(y, 2), x * 2 + lax.rem(y, 2), z * 2 + core)


def kernel(
    tokens_in, ids, units, weights, out_grad_in,
    moe_out, token_grad, weight_grad,
    full, term, reduced, row_send, grad_send, row_recv, grad_recv,
    res_send, back_send, res_recv, back_recv, rows, grads, act, gate_grad, up_grad,
    pick, weigh, tokens, out_grad, moe_sum, grad_sum,
    out_s, out_r, ret_s, ret_r, ag_s, ag_r, rs_s, rs_r, in_s, done_s,
):
    x, y, z, core = place()
    width = tokens.shape[1]
    hidden = weights.shape[2]
    token_count = tokens.shape[0]

    def peer(slot, sign):
        dz, dc = OFFSETS[slot]
        return device(x, y, lax.rem(z + (sign * dz) % 8, 8), lax.rem(core + dc, 2))

    def near(axis, step):
        if axis == 0:
            return device(lax.rem(x + step % 4, 4), y, z, core)
        return device(x, lax.rem(y + step % 4, 4), z, core)

    def block(half, first, second):
        dx, dy = (first, second) if half == 0 else (second, first)
        bx, by = lax.rem(x + dx % 4, 4), lax.rem(y + dy % 4, 4)
        return lax.div(by, 2) * 8 + bx * 2 + lax.rem(by, 2)

    barrier = pltpu.get_barrier_semaphore()
    for slot in range(1, SLOTS):
        pl.semaphore_signal(barrier, inc=1, device_id=peer(slot, 1), device_id_type=MESH)
    for axis in (0, 1):
        for step in (1, -1):
            pl.semaphore_signal(barrier, inc=1, device_id=near(axis, step), device_id_type=MESH)

    mine = block(0, 0, 0)
    loads = [
        pltpu.make_async_copy(src, dst, in_s.at[i])
        for i, (src, dst) in enumerate(
            ((tokens_in, tokens), (weights, full.at[mine]), (out_grad_in, out_grad))
        )
    ]
    for load in loads:
        load.start()

    shape = (ROWS, token_count)
    row = lax.broadcasted_iota(jnp.int32, shape, 0)
    slot_of = (row * 2731) >> 16
    rank_of = (row - slot_of * CAP).astype(F32)
    pair = slot_of >> 1
    dz = jnp.where((pair & 1) == 1, (pair + 1) >> 1, (8 - (pair >> 1)) & 7)
    named = ((z + dz) & 7) * 2 + ((core + slot_of) & 1)
    chosen = jnp.zeros(shape, F32)
    for k in range(ids.shape[0]):
        chosen = chosen + jnp.where(
            ids[k : k + 1, :] == named, units[k : k + 1, :].astype(F32), 0.0
        )
    earlier = (
        lax.broadcasted_iota(jnp.int32, (token_count, token_count), 0)
        < lax.broadcasted_iota(jnp.int32, (token_count, token_count), 1)
    ).astype(F32).astype(BF16)
    ranking = jnp.dot(
        (chosen > 0.0).astype(F32).astype(BF16), earlier, preferred_element_type=F32
    )
    gate = jnp.where(ranking == rank_of, chosen, 0.0)
    weigh[...] = (gate * (1.0 / 256.0)).astype(BF16)
    pick[...] = (gate > 0.0).astype(F32).astype(BF16)

    pl.semaphore_wait(barrier, SLOTS - 1 + 4)

    sent = []

    def send(src, dst, send_sem, recv_sem, to):
        copy = pltpu.make_async_remote_copy(
            src_ref=src, dst_ref=dst, send_sem=send_sem, recv_sem=recv_sem,
            device_id=to, device_id_type=MESH,
        )
        copy.start()
        sent.append(copy)
        return copy

    ag = {}

    def part(which, half):
        base = 64 * half
        return {"w": pl.ds(base, 64), "p": pl.ds(base, 32), "q": pl.ds(base + 32, 32)}[which]

    def gather_send(half, index, at, which, axis, step):
        ref = full.at[at, :, part(which, half), :]
        ag[half, index] = send(ref, ref, ag_s.at[half, index], ag_r.at[half, index], near(axis, step))

    ITEMS = (0, -1, 1, 2)

    def gather_own(half):
        a1, a2 = (0, 1) if half == 0 else (1, 0)
        gather_send(half, 0, mine, "w", a1, 1)
        gather_send(half, 1, mine, "w", a1, -1)

    def gather_item(half, k):
        a2 = 1 if half == 0 else 0
        at = block(half, ITEMS[k], 0)
        gather_send(half, 4 + 4 * k, at, "w", a2, 1)
        gather_send(half, 5 + 4 * k, at, "w", a2, -1)

    def gather_forward_first(half):
        a1 = 0 if half == 0 else 1
        ag[half, 0].wait_recv()
        gather_send(half, 2, block(half, -1, 0), "p", a1, 1)
        ag[half, 1].wait_recv()
        gather_send(half, 3, block(half, 1, 0), "q", a1, -1)

    def gather_forward_item(half, k):
        a2 = 1 if half == 0 else 0
        ag[half, 4 + 4 * k].wait_recv()
        gather_send(half, 6 + 4 * k, block(half, ITEMS[k], -1), "p", a2, 1)
        ag[half, 5 + 4 * k].wait_recv()
        gather_send(half, 7 + 4 * k, block(half, ITEMS[k], 1), "q", a2, -1)

    loads[1].wait()
    for half in (0, 1):
        gather_own(half)
    for half in (0, 1):
        gather_item(half, 0)

    out = {}

    def dispatch(lo, hi):
        cols = 512
        for a, (table, source, src, dst) in enumerate(
            ((pick, tokens, row_send, row_recv), (weigh, out_grad, grad_send, grad_recv))
        ):
            if (lo, hi) == PIECES[0]:
                loads[2 * a].wait()

            def tile(i, _, table=table, source=source, src=src):
                at = pl.ds(pl.multiple_of(i * cols, cols), cols)
                got = jnp.dot(
                    table[CAP * lo : CAP * hi, :], source[:, at], preferred_element_type=F32
                )
                src[lo:hi, :, at] = got.reshape(hi - lo, CAP, cols).astype(BF16)
                return 0

            lax.fori_loop(0, width // cols, tile, 0)
            for slot in range(max(lo, 1), hi):
                out[a, slot] = send(
                    src.at[slot], dst.at[slot], out_s.at[a, slot], out_r.at[a, slot], peer(slot, 1)
                )
            if lo == 0:
                dst[0] = src[0]

    for piece in PIECES:
        dispatch(*piece)
    for half in (0, 1):
        gather_forward_first(half)
    for half in (0, 1):
        gather_item(half, 1)
        gather_item(half, 2)
    for half in (0, 1):
        gather_forward_item(half, 0)
    for half in (0, 1):
        ag[half, 2].wait_recv()
        ag[half, 3].wait_recv()
        gather_item(half, 3)
    for k in (1, 2, 3):
        for half in (0, 1):
            gather_forward_item(half, k)
    for k in range(4):
        for half in (0, 1):
            ag[half, 6 + 4 * k].wait_recv()
            ag[half, 7 + 4 * k].wait_recv()

    ret = {}
    nt = (((1,), (1,)), ((), ()))
    tn = (((0,), (0,)), ((), ()))

    def experts(lo, hi):
        r0, r1 = CAP * lo, CAP * hi
        for slot in range(max(lo, 1), hi):
            for a in (0, 1):
                out[a, slot].wait_recv()

        def pack(i, _):
            at = pl.ds(pl.multiple_of(i * 512, 512), 512)
            for src, dst in ((row_recv, rows), (grad_recv, grads)):
                dst[r0:r1, at] = src[lo:hi, :, at].astype(F32).reshape(r1 - r0, 512).astype(BF16)
            return 0

        lax.fori_loop(0, width // 512, pack, 0)

        def inner(i, _):
            at = pl.ds(pl.multiple_of(i * 256, 256), 256)
            w = [full[:, j, :, at].reshape(width, 256) for j in range(3)]
            g = jnp.dot(rows[r0:r1, :], w[0], preferred_element_type=F32)
            u = jnp.dot(rows[r0:r1, :], w[1], preferred_element_type=F32)
            hg = jnp.dot(grads[r0:r1, :], w[2], preferred_element_type=F32)
            s = jax.nn.sigmoid(g)
            swish = g * s
            act[r0:r1, at] = (swish * u).astype(BF16)
            gate_grad[r0:r1, at] = (hg * u * s * (1.0 + g * (1.0 - s))).astype(BF16)
            up_grad[r0:r1, at] = (hg * swish).astype(BF16)
            return 0

        lax.fori_loop(0, hidden // 256, inner, 0)

        def outer(i, _):
            at = pl.ds(pl.multiple_of(i * 256, 256), 256)
            w = [full[pl.ds(2 * i, 2), j].reshape(256, hidden) for j in range(3)]
            res = lax.dot_general(act[r0:r1, :], w[2], nt, preferred_element_type=F32)
            res_send[lo:hi, :, at] = res.reshape(hi - lo, CAP, 256).astype(BF16)
            back = lax.dot_general(gate_grad[r0:r1, :], w[0], nt, preferred_element_type=F32)
            back = back + lax.dot_general(up_grad[r0:r1, :], w[1], nt, preferred_element_type=F32)
            back_send[lo:hi, :, at] = back.reshape(hi - lo, CAP, 256).astype(BF16)
            return 0

        lax.fori_loop(0, width // 256, outer, 0)
        for slot in range(max(lo, 1), hi):
            for a, (src, dst) in enumerate(((res_send, res_recv), (back_send, back_recv))):
                ret[a, slot] = send(
                    src.at[slot], dst.at[slot], ret_s.at[a, slot], ret_r.at[a, slot], peer(slot, -1)
                )
        if lo == 0:
            res_recv[0] = res_send[0]
            back_recv[0] = back_send[0]

    for lo, hi in CHUNKS:
        experts(lo, hi)

    def terms(i, _):
        at = pl.ds(pl.multiple_of(i * 256, 256), 256)
        for j, (left, right) in enumerate(((rows, gate_grad), (rows, up_grad), (grads, act))):
            got = lax.dot_general(left[:, at], right[...], tn, preferred_element_type=F32)
            term[pl.ds(2 * i, 2), j] = got.reshape(2, 128, hidden).astype(BF16)
        return 0

    lax.fori_loop(0, width // 256, terms, 0)

    rs = {}

    def reduce_send(half, index, at, which, axis, step):
        rs[half, index] = send(
            term.at[at, :, part(which, half), :], reduced.at[half, index],
            rs_s.at[half, index], rs_r.at[half, index], near(axis, step),
        )

    def add_into(half, at, which, indices):
        rows_at = part(which, half)
        for j in range(3):
            total = term[at, j, rows_at, :].astype(F32)
            for index in indices:
                total = total + reduced[half, index, j].astype(F32)
            term[at, j, rows_at, :] = total.astype(BF16)

    def ring(half, base, axis, at):
        def start():
            reduce_send(half, base + 0, at(2), "q", axis, 1)
            reduce_send(half, base + 1, at(2), "p", axis, -1)
            reduce_send(half, base + 2, at(1), "p", axis, 1)
            reduce_send(half, base + 3, at(-1), "q", axis, -1)

        def forward():
            rs[half, base + 0].wait_recv()
            add_into(half, at(1), "q", (base + 0,))
            reduce_send(half, base + 4, at(1), "q", axis, 1)
            rs[half, base + 1].wait_recv()
            add_into(half, at(-1), "p", (base + 1,))
            reduce_send(half, base + 5, at(-1), "p", axis, -1)

        def finish():
            for index in (2, 5):
                rs[half, base + index].wait_recv()
            add_into(half, at(0), "p", (base + 2, base + 5))
            for index in (3, 4):
                rs[half, base + index].wait_recv()
            add_into(half, at(0), "q", (base + 3, base + 4))

        return start, forward, finish

    first = {}
    ORDER = (2, 1, -1, 0)
    for k, i in enumerate(ORDER):
        for half in (0, 1):
            first[half, k] = ring(
                half, 6 * k, 1 if half == 0 else 0, functools.partial(block, half, i)
            )
    second = {
        half: ring(half, 24, 0 if half == 0 else 1, lambda j, half=half: block(half, j, 0))
        for half in (0, 1)
    }
    tables = ((weigh, res_recv, moe_sum, tokens, moe_out), (pick, back_recv, grad_sum, out_grad, token_grad))

    def combine(n):
        lo, hi = CHUNKS[n]
        r0, r1 = CAP * lo, CAP * hi
        for slot in range(max(lo, 1), hi):
            for a in (0, 1):
                ret[a, slot].wait_recv()

        def tile(i, _):
            at = pl.ds(pl.multiple_of(i * 256, 256), 256)
            for table, source, total, result, _ in tables:
                got = source[lo:hi, :, at].astype(F32).reshape(r1 - r0, 256).astype(BF16)
                value = lax.dot_general(table[r0:r1, :], got, tn, preferred_element_type=F32)
                if n > 0:
                    value = total[:, at] + value
                if hi < SLOTS:
                    total[:, at] = value
                else:
                    result[:, at] = value.astype(BF16)
            return 0

        if hi < SLOTS:
            lax.fori_loop(0, width // 256, tile, 0)
            return
        per = width // 256 // 4
        for part in range(4):
            lax.fori_loop(part * per, (part + 1) * per, tile, 0)
            at = pl.ds(part * per * 256, per * 256)
            for a, (_, _, _, result, to) in enumerate(tables):
                copy = pltpu.make_async_copy(result.at[:, at], to.at[:, at], done_s.at[a, part])
                copy.start()
                finals.append(copy)

    finals = []
    for stage in (0, 1):
        for k in range(4):
            for half in (0, 1):
                first[half, k][stage]()
    combine(0)
    for k in range(4):
        for half in (0, 1):
            first[half, k][2]()
    for stage in (0, 1, 2):
        for half in (0, 1):
            second[half][stage]()
    copy = pltpu.make_async_copy(term.at[mine], weight_grad, done_s.at[2, 0])
    copy.start()
    finals.append(copy)
    combine(1)
    combine(2)
    for copy in finals:
        copy.wait()
    for copy in sent:
        copy.wait_send()


def hand_out(*refs):
    sources, targets, (held_a, held_b, held_c, sems) = refs[:3], refs[3:6], refs[6:]
    steps = []
    for i, (src, held, dst) in enumerate(zip(sources, (held_a, held_b, held_c), targets)):
        parts = 4 if src.shape[0] % 4 == 0 else 3
        size = src.shape[0] // parts
        for k in range(parts):
            at = pl.ds(k * size, size)
            steps.append(
                (
                    pltpu.make_async_copy(src.at[at], held.at[at], sems.at[0, i, k]),
                    pltpu.make_async_copy(held.at[at], dst.at[at], sems.at[1, i, k]),
                )
            )
    for load, _ in steps:
        load.start()
    for load, store in steps:
        load.wait()
        store.start()
    for _, store in steps:
        store.wait()


def on_device(tokens, expert_ids, gate_units, expert_weights, out_grad):
    count, width = tokens.shape
    _, part, kinds, hidden = expert_weights.shape
    blocks = width // part
    vmem = pl.BlockSpec(memory_space=pltpu.VMEM)
    anywhere = pl.BlockSpec(memory_space=pl.ANY)
    slots = pltpu.VMEM((SLOTS, CAP, width), BF16)
    sem = pltpu.SemaphoreType.DMA
    shapes = (
        jax.ShapeDtypeStruct((count, width), BF16),
        jax.ShapeDtypeStruct((count, width), BF16),
        jax.ShapeDtypeStruct((kinds, part, hidden), BF16),
    )
    results = pl.pallas_call(
        kernel,
        out_shape=shapes,
        in_specs=[anywhere, vmem, vmem, anywhere, anywhere],
        out_specs=(anywhere,) * 3,
        scratch_shapes=[
            pltpu.VMEM((blocks, kinds, part, hidden), BF16),
            pltpu.VMEM((blocks, kinds, part, hidden), BF16),
            pltpu.VMEM((2, 30, kinds, part // 4, hidden), BF16),
            *([slots] * 8),
            *([pltpu.VMEM((ROWS, width), BF16)] * 2),
            *([pltpu.VMEM((ROWS, hidden), BF16)] * 3),
            *([pltpu.VMEM((ROWS, count), BF16)] * 2),
            *([pltpu.VMEM((count, width), BF16)] * 2),
            *([pltpu.VMEM((count, width), F32)] * 2),
            sem((2, SLOTS)), sem((2, SLOTS)), sem((2, SLOTS)), sem((2, SLOTS)),
            sem((2, 20)), sem((2, 20)), sem((2, 30)), sem((2, 30)), sem((3,)), sem((3, 4)),
        ],
        compiler_params=pltpu.CompilerParams(
            collective_id=0, has_side_effects=True, vmem_limit_bytes=62 * 1024 * 1024
        ),
        name="experts",
    )(tokens, expert_ids.T, gate_units.T, jnp.transpose(expert_weights[0], (1, 0, 2)), out_grad)
    moe_out, token_grad, weight_grad = pl.pallas_call(
        hand_out,
        out_shape=shapes,
        in_specs=[anywhere] * 3,
        out_specs=(anywhere,) * 3,
        scratch_shapes=[*(pltpu.VMEM(a.shape, a.dtype) for a in shapes), sem((2, 3, 4))],
        name="hand_out",
    )(*results)
    return moe_out, token_grad, jnp.transpose(weight_grad, (1, 0, 2))[None]


def solution(mesh):
    rows = P(("dp", "fsdp", "expert"), None)
    split = P("expert", ("dp", "fsdp"), None, None)
    return jax.shard_map(
        on_device,
        mesh=mesh,
        in_specs=(rows, rows, rows, split, rows),
        out_specs=(rows, rows, split),
        check_vma=False,
    )
```

```python
import functools

import jax
import jax.numpy as jnp
from jax import lax
from jax.experimental import pallas as pl
from jax.experimental.pallas import tpu as pltpu
from jax.sharding import PartitionSpec as P

CAP = 24
SLOTS = 16
ROWS = CAP * SLOTS
MESH = pl.DeviceIdType.MESH
BF16 = jnp.bfloat16
F32 = jnp.float32

OFFSETS = [(dz, dc) for dz in (0, 1, 7, 2, 6, 3, 5, 4) for dc in (0, 1)]
CHUNKS = ((0, 10), (10, 14), (14, 16))
PIECES = ((2, 6), (6, 10), (10, 14), (14, 16), (0, 2))


def place():
    dp, fsdp, expert = (lax.axis_index(n) for n in ("dp", "fsdp", "expert"))
    return lax.div(fsdp, 2), dp * 2 + lax.rem(fsdp, 2), lax.div(expert, 2), lax.rem(expert, 2)


def device(x, y, z, core):
    return (lax.div(y, 2), x * 2 + lax.rem(y, 2), z * 2 + core)


def kernel(
    tokens_in, ids, units, weights, out_grad_in,
    moe_out, token_grad, weight_grad,
    full, term, reduced, row_send, grad_send, row_recv, grad_recv,
    res_send, back_send, res_recv, back_recv, rows, grads, act, gate_grad, up_grad,
    pick, weigh, tokens, out_grad, moe_sum, grad_sum, spread_a, spread_b, spread_c,
    out_s, out_r, ret_s, ret_r, ag_s, ag_r, rs_s, rs_r, in_s,
):
    x, y, z, core = place()
    width = tokens.shape[1]
    hidden = weights.shape[2]
    token_count = tokens.shape[0]

    def peer(slot, sign):
        dz, dc = OFFSETS[slot]
        return device(x, y, lax.rem(z + (sign * dz) % 8, 8), lax.rem(core + dc, 2))

    def near(axis, step):
        if axis == 0:
            return device(lax.rem(x + step % 4, 4), y, z, core)
        return device(x, lax.rem(y + step % 4, 4), z, core)

    def block(half, first, second):
        dx, dy = (first, second) if half == 0 else (second, first)
        bx, by = lax.rem(x + dx % 4, 4), lax.rem(y + dy % 4, 4)
        return lax.div(by, 2) * 8 + bx * 2 + lax.rem(by, 2)

    barrier = pltpu.get_barrier_semaphore()
    for slot in range(1, SLOTS):
        pl.semaphore_signal(barrier, inc=1, device_id=peer(slot, 1), device_id_type=MESH)
    for axis in (0, 1):
        for step in (1, -1):
            pl.semaphore_signal(barrier, inc=1, device_id=near(axis, step), device_id_type=MESH)

    mine = block(0, 0, 0)
    loads = [
        pltpu.make_async_copy(src, dst, in_s.at[i])
        for i, (src, dst) in enumerate(
            ((tokens_in, tokens), (weights, full.at[mine]), (out_grad_in, out_grad))
        )
    ]
    for load in loads:
        load.start()

    shape = (ROWS, token_count)
    row = lax.broadcasted_iota(jnp.int32, shape, 0)
    slot_of = (row * 2731) >> 16
    rank_of = (row - slot_of * CAP).astype(F32)
    pair = slot_of >> 1
    dz = jnp.where((pair & 1) == 1, (pair + 1) >> 1, (8 - (pair >> 1)) & 7)
    named = ((z + dz) & 7) * 2 + ((core + slot_of) & 1)
    chosen = jnp.zeros(shape, F32)
    for k in range(ids.shape[0]):
        chosen = chosen + jnp.where(
            ids[k : k + 1, :] == named, units[k : k + 1, :].astype(F32), 0.0
        )
    earlier = (
        lax.broadcasted_iota(jnp.int32, (token_count, token_count), 0)
        < lax.broadcasted_iota(jnp.int32, (token_count, token_count), 1)
    ).astype(F32).astype(BF16)
    ranking = jnp.dot(
        (chosen > 0.0).astype(F32).astype(BF16), earlier, preferred_element_type=F32
    )
    gate = jnp.where(ranking == rank_of, chosen, 0.0)
    weigh[...] = (gate * (1.0 / 256.0)).astype(BF16)
    pick[...] = (gate > 0.0).astype(F32).astype(BF16)

    pl.semaphore_wait(barrier, SLOTS - 1 + 4)

    sent = []

    def send(src, dst, send_sem, recv_sem, to):
        copy = pltpu.make_async_remote_copy(
            src_ref=src, dst_ref=dst, send_sem=send_sem, recv_sem=recv_sem,
            device_id=to, device_id_type=MESH,
        )
        copy.start()
        sent.append(copy)
        return copy

    ag = {}

    def part(which, half):
        base = 64 * half
        return {"w": pl.ds(base, 64), "p": pl.ds(base, 32), "q": pl.ds(base + 32, 32)}[which]

    def gather_send(half, index, at, which, axis, step):
        ref = full.at[at, :, part(which, half), :]
        ag[half, index] = send(ref, ref, ag_s.at[half, index], ag_r.at[half, index], near(axis, step))

    ITEMS = (0, -1, 1, 2)

    def gather_own(half):
        a1, a2 = (0, 1) if half == 0 else (1, 0)
        gather_send(half, 0, mine, "w", a1, 1)
        gather_send(half, 1, mine, "w", a1, -1)

    def gather_item(half, k):
        a2 = 1 if half == 0 else 0
        at = block(half, ITEMS[k], 0)
        gather_send(half, 4 + 4 * k, at, "w", a2, 1)
        gather_send(half, 5 + 4 * k, at, "w", a2, -1)

    def gather_forward_first(half):
        a1 = 0 if half == 0 else 1
        ag[half, 0].wait_recv()
        gather_send(half, 2, block(half, -1, 0), "p", a1, 1)
        ag[half, 1].wait_recv()
        gather_send(half, 3, block(half, 1, 0), "q", a1, -1)

    def gather_forward_item(half, k):
        a2 = 1 if half == 0 else 0
        ag[half, 4 + 4 * k].wait_recv()
        gather_send(half, 6 + 4 * k, block(half, ITEMS[k], -1), "p", a2, 1)
        ag[half, 5 + 4 * k].wait_recv()
        gather_send(half, 7 + 4 * k, block(half, ITEMS[k], 1), "q", a2, -1)

    loads[1].wait()
    for half in (0, 1):
        gather_own(half)
    for half in (0, 1):
        gather_item(half, 0)

    out = {}

    def dispatch(lo, hi):
        cols = 512
        for a, (table, source, src, dst) in enumerate(
            ((pick, tokens, row_send, row_recv), (weigh, out_grad, grad_send, grad_recv))
        ):
            if (lo, hi) == PIECES[0]:
                loads[2 * a].wait()

            def tile(i, _, table=table, source=source, src=src):
                at = pl.ds(pl.multiple_of(i * cols, cols), cols)
                got = jnp.dot(
                    table[CAP * lo : CAP * hi, :], source[:, at], preferred_element_type=F32
                )
                src[lo:hi, :, at] = got.reshape(hi - lo, CAP, cols).astype(BF16)
                return 0

            lax.fori_loop(0, width // cols, tile, 0, unroll=(lo, hi) == PIECES[0])
            for slot in range(max(lo, 1), hi):
                out[a, slot] = send(
                    src.at[slot], dst.at[slot], out_s.at[a, slot], out_r.at[a, slot], peer(slot, 1)
                )
            if lo == 0:
                dst[0] = src[0]

    for piece in PIECES:
        dispatch(*piece)
    spread = (spread_a, spread_b, spread_c)
    for (lo, hi), to in zip(CHUNKS, spread):
        for a, table in enumerate((weigh, pick)):
            to[a] = jnp.transpose(table[CAP * lo : CAP * hi, :].astype(F32)).astype(BF16)
    for half in (0, 1):
        gather_forward_first(half)
    for half in (0, 1):
        gather_item(half, 1)
        gather_item(half, 2)
    for half in (0, 1):
        gather_forward_item(half, 0)
    for half in (0, 1):
        ag[half, 2].wait_recv()
        ag[half, 3].wait_recv()
        gather_item(half, 3)
    for k in (1, 2, 3):
        for half in (0, 1):
            gather_forward_item(half, k)
    for k in range(4):
        for half in (0, 1):
            ag[half, 6 + 4 * k].wait_recv()
            ag[half, 7 + 4 * k].wait_recv()

    ret = {}
    nt = (((1,), (1,)), ((), ()))
    tn = (((0,), (0,)), ((), ()))

    def experts(lo, hi):
        r0, r1 = CAP * lo, CAP * hi
        for slot in range(max(lo, 1), hi):
            for a in (0, 1):
                out[a, slot].wait_recv()

        def pack(i, _):
            at = pl.ds(pl.multiple_of(i * 512, 512), 512)
            for src, dst in ((row_recv, rows), (grad_recv, grads)):
                dst[r0:r1, at] = src[lo:hi, :, at].astype(F32).reshape(r1 - r0, 512).astype(BF16)
            return 0

        lax.fori_loop(0, width // 512, pack, 0)

        def inner(i, _):
            at = pl.ds(pl.multiple_of(i * 256, 256), 256)
            w = [full[:, j, :, at].reshape(width, 256) for j in range(3)]
            g = jnp.dot(rows[r0:r1, :], w[0], preferred_element_type=F32)
            u = jnp.dot(rows[r0:r1, :], w[1], preferred_element_type=F32)
            hg = jnp.dot(grads[r0:r1, :], w[2], preferred_element_type=F32)
            s = jax.nn.sigmoid(g)
            swish = g * s
            act[r0:r1, at] = (swish * u).astype(BF16)
            gate_grad[r0:r1, at] = (hg * u * s * (1.0 + g * (1.0 - s))).astype(BF16)
            up_grad[r0:r1, at] = (hg * swish).astype(BF16)
            return 0

        lax.fori_loop(0, hidden // 256, inner, 0)

        def outer(i, _):
            at = pl.ds(pl.multiple_of(i * 256, 256), 256)
            w = [full[pl.ds(2 * i, 2), j].reshape(256, hidden) for j in range(3)]
            res = lax.dot_general(act[r0:r1, :], w[2], nt, preferred_element_type=F32)
            res_send[lo:hi, :, at] = res.reshape(hi - lo, CAP, 256).astype(BF16)
            back = lax.dot_general(gate_grad[r0:r1, :], w[0], nt, preferred_element_type=F32)
            back = back + lax.dot_general(up_grad[r0:r1, :], w[1], nt, preferred_element_type=F32)
            back_send[lo:hi, :, at] = back.reshape(hi - lo, CAP, 256).astype(BF16)
            return 0

        lax.fori_loop(0, width // 256, outer, 0)
        for slot in range(max(lo, 1), hi):
            for a, (src, dst) in enumerate(((res_send, res_recv), (back_send, back_recv))):
                ret[a, slot] = send(
                    src.at[slot], dst.at[slot], ret_s.at[a, slot], ret_r.at[a, slot], peer(slot, -1)
                )
        if lo == 0:
            res_recv[0] = res_send[0]
            back_recv[0] = back_send[0]

    for lo, hi in CHUNKS:
        experts(lo, hi)

    def terms(i, _):
        at = pl.ds(pl.multiple_of(i * 256, 256), 256)
        for j, (left, right) in enumerate(((rows, gate_grad), (rows, up_grad), (grads, act))):
            got = lax.dot_general(left[:, at], right[...], tn, preferred_element_type=F32)
            term[pl.ds(2 * i, 2), j] = got.reshape(2, 128, hidden).astype(BF16)
        return 0

    lax.fori_loop(0, width // 256, terms, 0)

    rs = {}

    def reduce_send(half, index, at, which, axis, step):
        rs[half, index] = send(
            term.at[at, :, part(which, half), :], reduced.at[half, index],
            rs_s.at[half, index], rs_r.at[half, index], near(axis, step),
        )

    def add_into(half, at, which, indices):
        rows_at = part(which, half)
        for j in range(3):
            total = term[at, j, rows_at, :].astype(F32)
            for index in indices:
                total = total + reduced[half, index, j].astype(F32)
            term[at, j, rows_at, :] = total.astype(BF16)

    def ring(half, base, axis, at):
        def start():
            reduce_send(half, base + 0, at(2), "q", axis, 1)
            reduce_send(half, base + 1, at(2), "p", axis, -1)
            reduce_send(half, base + 2, at(1), "p", axis, 1)
            reduce_send(half, base + 3, at(-1), "q", axis, -1)

        def forward():
            rs[half, base + 0].wait_recv()
            add_into(half, at(1), "q", (base + 0,))
            reduce_send(half, base + 4, at(1), "q", axis, 1)
            rs[half, base + 1].wait_recv()
            add_into(half, at(-1), "p", (base + 1,))
            reduce_send(half, base + 5, at(-1), "p", axis, -1)

        def finish():
            for index in (2, 5):
                rs[half, base + index].wait_recv()
            add_into(half, at(0), "p", (base + 2, base + 5))
            for index in (3, 4):
                rs[half, base + index].wait_recv()
            add_into(half, at(0), "q", (base + 3, base + 4))

        return start, forward, finish

    first = {}
    ORDER = (2, 1, -1, 0)
    for k, i in enumerate(ORDER):
        for half in (0, 1):
            first[half, k] = ring(
                half, 6 * k, 1 if half == 0 else 0, functools.partial(block, half, i)
            )
    second = {
        half: ring(half, 24, 0 if half == 0 else 1, lambda j, half=half: block(half, j, 0))
        for half in (0, 1)
    }
    tables = ((res_recv, moe_sum, moe_out), (back_recv, grad_sum, token_grad))

    def combine(n):
        lo, hi = CHUNKS[n]
        for slot in range(max(lo, 1), hi):
            for a in (0, 1):
                ret[a, slot].wait_recv()

        def tile(i, _):
            at = pl.ds(pl.multiple_of(i * 512, 512), 512)
            for a, (source, total, result) in enumerate(tables):
                got = source[lo:hi, :, at].astype(F32).reshape(CAP * (hi - lo), 512).astype(BF16)
                value = jnp.dot(spread[n][a], got, preferred_element_type=F32)
                if n > 0:
                    value = total[:, at] + value
                if hi < SLOTS:
                    total[:, at] = value
                else:
                    result[:, at] = value.astype(BF16)
            return 0

        lax.fori_loop(0, width // 512, tile, 0, unroll=hi == SLOTS)

    for stage in (0, 1):
        for k in range(4):
            for half in (0, 1):
                first[half, k][stage]()
    combine(0)
    for k in range(4):
        for half in (0, 1):
            first[half, k][2]()
    for stage in (0, 1, 2):
        for half in (0, 1):
            second[half][stage]()
    weight_grad[...] = term[mine]
    combine(1)
    combine(2)
    for copy in sent:
        copy.wait_send()


def hand_out(*refs):
    sources, targets, sems = refs[:3], refs[3:6], refs[6]
    copies = []
    for i, (src, dst) in enumerate(zip(sources, targets)):
        parts = 4 if src.shape[0] % 4 == 0 else 3
        size = src.shape[0] // parts
        for k in range(parts):
            at = pl.ds(k * size, size)
            copies.append(pltpu.make_async_copy(src.at[at], dst.at[at], sems.at[i, k]))
    for copy in copies:
        copy.start()
    for copy in copies:
        copy.wait()


def on_device(tokens, expert_ids, gate_units, expert_weights, out_grad):
    count, width = tokens.shape
    _, part, kinds, hidden = expert_weights.shape
    blocks = width // part
    vmem = pl.BlockSpec(memory_space=pltpu.VMEM)
    anywhere = pl.BlockSpec(memory_space=pl.ANY)
    slots = pltpu.VMEM((SLOTS, CAP, width), BF16)
    sem = pltpu.SemaphoreType.DMA
    shapes = (
        jax.ShapeDtypeStruct((count, width), BF16),
        jax.ShapeDtypeStruct((count, width), BF16),
        jax.ShapeDtypeStruct((kinds, part, hidden), BF16),
    )
    results = pl.pallas_call(
        kernel,
        out_shape=tuple(pltpu.VMEM(a.shape, a.dtype) for a in shapes),
        in_specs=[anywhere, vmem, vmem, anywhere, anywhere],
        out_specs=(vmem,) * 3,
        scratch_shapes=[
            pltpu.VMEM((blocks, kinds, part, hidden), BF16),
            pltpu.VMEM((blocks, kinds, part, hidden), BF16),
            pltpu.VMEM((2, 30, kinds, part // 4, hidden), BF16),
            *([slots] * 8),
            *([pltpu.VMEM((ROWS, width), BF16)] * 2),
            *([pltpu.VMEM((ROWS, hidden), BF16)] * 3),
            *([pltpu.VMEM((ROWS, count), BF16)] * 2),
            *([pltpu.VMEM((count, width), BF16)] * 2),
            *([pltpu.VMEM((count, width), F32)] * 2),
            *(pltpu.VMEM((2, count, CAP * (hi - lo)), BF16) for lo, hi in CHUNKS),
            sem((2, SLOTS)), sem((2, SLOTS)), sem((2, SLOTS)), sem((2, SLOTS)),
            sem((2, 20)), sem((2, 20)), sem((2, 30)), sem((2, 30)), sem((3,)),
        ],
        compiler_params=pltpu.CompilerParams(
            collective_id=0, has_side_effects=True, vmem_limit_bytes=57 * 1024 * 1024
        ),
        name="experts",
    )(tokens, expert_ids.T, gate_units.T, jnp.transpose(expert_weights[0], (1, 0, 2)), out_grad)
    moe_out, token_grad, weight_grad = pl.pallas_call(
        hand_out,
        out_shape=shapes,
        in_specs=[anywhere] * 3,
        out_specs=(anywhere,) * 3,
        scratch_shapes=[sem((3, 4))],
        name="hand_out",
    )(*(pltpu.with_memory_space_constraint(a, pltpu.VMEM) for a in results))
    return moe_out, token_grad, jnp.transpose(weight_grad, (1, 0, 2))[None]


def solution(mesh):
    rows = P(("dp", "fsdp", "expert"), None)
    split = P("expert", ("dp", "fsdp"), None, None)
    return jax.shard_map(
        on_device,
        mesh=mesh,
        in_specs=(rows, rows, rows, split, rows),
        out_specs=(rows, rows, split),
        check_vma=False,
    )
```

```python
import functools

import jax
import jax.numpy as jnp
from jax import lax
from jax.experimental import pallas as pl
from jax.experimental.pallas import tpu as pltpu
from jax.sharding import PartitionSpec as P

CAP = 24
SLOTS = 16
ROWS = CAP * SLOTS
MESH = pl.DeviceIdType.MESH
BF16 = jnp.bfloat16
F32 = jnp.float32

STEPS = (0, 1, 7, 2, 6, 3, 5, 4)
OFFSETS = [(dz, dc) for dz in STEPS for dc in (0, 1)]
OWN = OFFSETS.index((0, 0))
CHUNKS = ((0, 10), (10, 14), (14, 16))
PIECES = ((2, 4), (4, 6), (6, 10), (10, 14), (14, 16), (0, 2))


def place():
    dp, fsdp, expert = (lax.axis_index(n) for n in ("dp", "fsdp", "expert"))
    return lax.div(fsdp, 2), dp * 2 + lax.rem(fsdp, 2), lax.div(expert, 2), lax.rem(expert, 2)


def device(x, y, z, core):
    return (lax.div(y, 2), x * 2 + lax.rem(y, 2), z * 2 + core)


def others(lo, hi):
    return [slot for slot in range(lo, hi) if slot != OWN]


def kernel(
    tokens_in, ids, units, weights, out_grad_in,
    moe_out, token_grad, weight_grad,
    full, term, reduced, pair_send, pair_recv, ret_send, ret_recv, rows, grads, act, gate_grad, up_grad,
    pick, weigh, tokens, out_grad, moe_sum, grad_sum, spread_a, spread_b, spread_c,
    out_s, out_r, ret_s, ret_r, ag_s, ag_r, rs_s, rs_r, in_s,
):
    x, y, z, core = place()
    (row_send, grad_send), (row_recv, grad_recv), (res_send, back_send), (res_recv, back_recv) = (
        (ref.at[:, 0], ref.at[:, 1]) for ref in (pair_send, pair_recv, ret_send, ret_recv)
    )
    width = tokens.shape[1]
    hidden = weights.shape[2]
    token_count = tokens.shape[0]

    def peer(slot, sign):
        dz, dc = OFFSETS[slot]
        return device(x, y, lax.rem(z + (sign * dz) % 8, 8), lax.rem(core + dc, 2))

    def near(axis, step):
        if axis == 0:
            return device(lax.rem(x + step % 4, 4), y, z, core)
        return device(x, lax.rem(y + step % 4, 4), z, core)

    def block(half, first, second):
        dx, dy = (first, second) if half == 0 else (second, first)
        bx, by = lax.rem(x + dx % 4, 4), lax.rem(y + dy % 4, 4)
        return lax.div(by, 2) * 8 + bx * 2 + lax.rem(by, 2)

    barrier = pltpu.get_barrier_semaphore()
    for slot in others(0, SLOTS):
        pl.semaphore_signal(barrier, inc=1, device_id=peer(slot, 1), device_id_type=MESH)
    for axis in (0, 1):
        for step in (1, -1):
            pl.semaphore_signal(barrier, inc=1, device_id=near(axis, step), device_id_type=MESH)

    mine = block(0, 0, 0)
    loads = [
        pltpu.make_async_copy(src, dst, in_s.at[i])
        for i, (src, dst) in enumerate(
            ((tokens_in, tokens), (weights, full.at[mine]), (out_grad_in, out_grad))
        )
    ]
    for load in loads:
        load.start()

    shape = (ROWS, token_count)
    row = lax.broadcasted_iota(jnp.int32, shape, 0)
    slot_of = (row * 2731) >> 16
    rank_of = (row - slot_of * CAP).astype(F32)
    pair = slot_of >> 1
    dz = jnp.zeros(shape, jnp.int32)
    for k, step in enumerate(STEPS):
        dz = jnp.where(pair == k, step, dz)
    named = ((z + dz) & 7) * 2 + ((core + slot_of) & 1)
    chosen = jnp.zeros(shape, F32)
    for k in range(ids.shape[0]):
        chosen = chosen + jnp.where(
            ids[k : k + 1, :] == named, units[k : k + 1, :].astype(F32), 0.0
        )
    earlier = (
        lax.broadcasted_iota(jnp.int32, (token_count, token_count), 0)
        < lax.broadcasted_iota(jnp.int32, (token_count, token_count), 1)
    ).astype(F32).astype(BF16)
    ranking = jnp.dot(
        (chosen > 0.0).astype(F32).astype(BF16), earlier, preferred_element_type=F32
    )
    gate = jnp.where(ranking == rank_of, chosen, 0.0)
    weigh[...] = (gate * (1.0 / 256.0)).astype(BF16)
    pick[...] = (gate > 0.0).astype(F32).astype(BF16)

    sent = []

    def send(src, dst, send_sem, recv_sem, to):
        copy = pltpu.make_async_remote_copy(
            src_ref=src, dst_ref=dst, send_sem=send_sem, recv_sem=recv_sem,
            device_id=to, device_id_type=MESH,
        )
        copy.start()
        sent.append(copy)
        return copy

    ag = {}

    def part(which, half):
        base = 64 * half
        return {"w": pl.ds(base, 64), "p": pl.ds(base, 32), "q": pl.ds(base + 32, 32)}[which]

    def gather_send(half, index, at, which, axis, step):
        ref = full.at[at, :, part(which, half), :]
        ag[half, index] = send(ref, ref, ag_s.at[half, index], ag_r.at[half, index], near(axis, step))

    ITEMS = (0, -1, 1, 2)

    def gather_own(half):
        a1, a2 = (0, 1) if half == 0 else (1, 0)
        gather_send(half, 0, mine, "w", a1, 1)
        gather_send(half, 1, mine, "w", a1, -1)

    def gather_item(half, k):
        a2 = 1 if half == 0 else 0
        at = block(half, ITEMS[k], 0)
        gather_send(half, 4 + 4 * k, at, "w", a2, 1)
        gather_send(half, 5 + 4 * k, at, "w", a2, -1)

    def gather_forward_first(half):
        a1 = 0 if half == 0 else 1
        ag[half, 0].wait_recv()
        gather_send(half, 2, block(half, -1, 0), "p", a1, 1)
        ag[half, 1].wait_recv()
        gather_send(half, 3, block(half, 1, 0), "q", a1, -1)

    def gather_forward_item(half, k):
        a2 = 1 if half == 0 else 0
        ag[half, 4 + 4 * k].wait_recv()
        gather_send(half, 6 + 4 * k, block(half, ITEMS[k], -1), "p", a2, 1)
        ag[half, 5 + 4 * k].wait_recv()
        gather_send(half, 7 + 4 * k, block(half, ITEMS[k], 1), "q", a2, -1)

    out = {}
    routes = ((pick, tokens, row_send, row_recv), (weigh, out_grad, grad_send, grad_recv))

    def choose(piece, a):
        lo, hi = piece
        cols = 512
        table, source, src, _ = routes[a]
        if piece == PIECES[0]:
            loads[2 * a].wait()

        def tile(i, _):
            at = pl.ds(pl.multiple_of(i * cols, cols), cols)
            got = jnp.dot(
                table[CAP * lo : CAP * hi, :], source[:, at], preferred_element_type=F32
            )
            src[lo:hi, :, at] = got.reshape(hi - lo, CAP, cols).astype(BF16)
            return 0

        lax.fori_loop(0, width // cols, tile, 0, unroll=piece == PIECES[0])

    def post(piece):
        lo, hi = piece
        for slot in others(lo, hi):
            out[slot] = send(
                pair_send.at[slot], pair_recv.at[slot], out_s.at[slot], out_r.at[slot], peer(slot, 1)
            )
        if lo <= OWN < hi:
            pair_recv[OWN] = pair_send[OWN]

    choose(PIECES[0], 0)
    choose(PIECES[0], 1)
    pl.semaphore_wait(barrier, SLOTS - 1 + 4)
    post(PIECES[0])
    loads[1].wait()
    for half in (0, 1):
        gather_own(half)
    for half in (0, 1):
        gather_item(half, 0)
    for piece in PIECES[1:]:
        choose(piece, 0)
        choose(piece, 1)
        post(piece)
    spread = (spread_a, spread_b, spread_c)
    for (lo, hi), to in zip(CHUNKS, spread):
        for a, table in enumerate((weigh, pick)):
            to[a] = jnp.transpose(table[CAP * lo : CAP * hi, :].astype(F32)).astype(BF16)
    for half in (0, 1):
        gather_forward_first(half)
    for half in (0, 1):
        gather_item(half, 1)
        gather_item(half, 2)
    for half in (0, 1):
        gather_forward_item(half, 0)
    for half in (0, 1):
        ag[half, 2].wait_recv()
        ag[half, 3].wait_recv()
        gather_item(half, 3)
    for k in (1, 2, 3):
        for half in (0, 1):
            gather_forward_item(half, k)
    for k in range(4):
        for half in (0, 1):
            ag[half, 6 + 4 * k].wait_recv()
            ag[half, 7 + 4 * k].wait_recv()

    ret = {}
    nt = (((1,), (1,)), ((), ()))
    tn = (((0,), (0,)), ((), ()))

    def experts(lo, hi):
        r0, r1 = CAP * lo, CAP * hi
        for slot in others(lo, hi):
            out[slot].wait_recv()

        def pack(i, _):
            at = pl.ds(pl.multiple_of(i * 512, 512), 512)
            for src, dst in ((row_recv, rows), (grad_recv, grads)):
                dst[r0:r1, at] = src[lo:hi, :, at].astype(F32).reshape(r1 - r0, 512).astype(BF16)
            return 0

        lax.fori_loop(0, width // 512, pack, 0)

        def inner(i, _):
            at = pl.ds(pl.multiple_of(i * 256, 256), 256)
            w = [full[:, j, :, at].reshape(width, 256) for j in range(3)]
            g = jnp.dot(rows[r0:r1, :], w[0], preferred_element_type=F32)
            u = jnp.dot(rows[r0:r1, :], w[1], preferred_element_type=F32)
            hg = jnp.dot(grads[r0:r1, :], w[2], preferred_element_type=F32)
            s = jax.nn.sigmoid(g)
            swish = g * s
            act[r0:r1, at] = (swish * u).astype(BF16)
            gate_grad[r0:r1, at] = (hg * u * s * (1.0 + g * (1.0 - s))).astype(BF16)
            up_grad[r0:r1, at] = (hg * swish).astype(BF16)
            return 0

        lax.fori_loop(0, hidden // 256, inner, 0)

        def outer(i, _):
            at = pl.ds(pl.multiple_of(i * 256, 256), 256)
            w = [full[pl.ds(2 * i, 2), j].reshape(256, hidden) for j in range(3)]
            res = lax.dot_general(act[r0:r1, :], w[2], nt, preferred_element_type=F32)
            res_send[lo:hi, :, at] = res.reshape(hi - lo, CAP, 256).astype(BF16)
            back = lax.dot_general(gate_grad[r0:r1, :], w[0], nt, preferred_element_type=F32)
            back = back + lax.dot_general(up_grad[r0:r1, :], w[1], nt, preferred_element_type=F32)
            back_send[lo:hi, :, at] = back.reshape(hi - lo, CAP, 256).astype(BF16)
            return 0

        lax.fori_loop(0, width // 256, outer, 0)
        for slot in others(lo, hi):
            ret[slot] = send(
                ret_send.at[slot], ret_recv.at[slot], ret_s.at[slot], ret_r.at[slot], peer(slot, -1)
            )
        if lo <= OWN < hi:
            ret_recv[OWN] = ret_send[OWN]

    for lo, hi in CHUNKS:
        experts(lo, hi)

    def terms(i, _):
        at = pl.ds(pl.multiple_of(i * 256, 256), 256)
        for j, (left, right) in enumerate(((rows, gate_grad), (rows, up_grad), (grads, act))):
            got = lax.dot_general(left[:, at], right[...], tn, preferred_element_type=F32)
            term[pl.ds(2 * i, 2), j] = got.reshape(2, 128, hidden).astype(BF16)
        return 0

    lax.fori_loop(0, width // 256, terms, 0)

    rs = {}

    def reduce_send(half, index, at, which, axis, step):
        rs[half, index] = send(
            term.at[at, :, part(which, half), :], reduced.at[half, index],
            rs_s.at[half, index], rs_r.at[half, index], near(axis, step),
        )

    def add_into(half, at, which, indices):
        rows_at = part(which, half)
        for j in range(3):
            total = term[at, j, rows_at, :].astype(F32)
            for index in indices:
                total = total + reduced[half, index, j].astype(F32)
            term[at, j, rows_at, :] = total.astype(BF16)

    def ring(half, base, axis, at):
        def start():
            reduce_send(half, base + 0, at(2), "q", axis, 1)
            reduce_send(half, base + 1, at(2), "p", axis, -1)
            reduce_send(half, base + 2, at(1), "p", axis, 1)
            reduce_send(half, base + 3, at(-1), "q", axis, -1)

        def forward():
            rs[half, base + 0].wait_recv()
            add_into(half, at(1), "q", (base + 0,))
            reduce_send(half, base + 4, at(1), "q", axis, 1)
            rs[half, base + 1].wait_recv()
            add_into(half, at(-1), "p", (base + 1,))
            reduce_send(half, base + 5, at(-1), "p", axis, -1)

        def finish():
            for index in (2, 5):
                rs[half, base + index].wait_recv()
            add_into(half, at(0), "p", (base + 2, base + 5))
            for index in (3, 4):
                rs[half, base + index].wait_recv()
            add_into(half, at(0), "q", (base + 3, base + 4))

        return start, forward, finish

    first = {}
    ORDER = (2, 1, -1, 0)
    for k, i in enumerate(ORDER):
        for half in (0, 1):
            first[half, k] = ring(
                half, 6 * k, 1 if half == 0 else 0, functools.partial(block, half, i)
            )
    second = {
        half: ring(half, 24, 0 if half == 0 else 1, lambda j, half=half: block(half, j, 0))
        for half in (0, 1)
    }
    tables = ((res_recv, moe_sum, moe_out), (back_recv, grad_sum, token_grad))

    def combine(n, a):
        lo, hi = CHUNKS[n]
        source, total, result = tables[a]
        if a == 0:
            for slot in others(lo, hi):
                ret[slot].wait_recv()

        def tile(i, _):
            at = pl.ds(pl.multiple_of(i * 512, 512), 512)
            got = source[lo:hi, :, at].astype(F32).reshape(CAP * (hi - lo), 512).astype(BF16)
            value = jnp.dot(spread[n][a], got, preferred_element_type=F32)
            if n > 0:
                value = total[:, at] + value
            if hi < SLOTS:
                total[:, at] = value
            else:
                result[:, at] = value.astype(BF16)
            return 0

        lax.fori_loop(0, width // 512, tile, 0, unroll=hi == SLOTS)

    for stage in (0, 1):
        for k in range(4):
            for half in (0, 1):
                first[half, k][stage]()
    for a in (0, 1):
        combine(0, a)
    for k in range(4):
        for half in (0, 1):
            first[half, k][2]()
    for stage in (0, 1, 2):
        for half in (0, 1):
            second[half][stage]()
    weight_grad[...] = term[mine]
    for n in (1, 2):
        for a in (0, 1):
            combine(n, a)
    for copy in sent:
        copy.wait_send()


def hand_out(*refs):
    sources, targets, sems = refs[:3], refs[3:6], refs[6]
    copies = []
    for i, (src, dst) in enumerate(zip(sources, targets)):
        parts = 2 if src.shape[0] % 2 == 0 else 1
        size = src.shape[0] // parts
        for k in range(parts):
            at = pl.ds(k * size, size)
            copies.append(pltpu.make_async_copy(src.at[at], dst.at[at], sems.at[i, k]))
    for copy in copies:
        copy.start()
    for copy in copies:
        copy.wait()


def on_device(tokens, expert_ids, gate_units, expert_weights, out_grad):
    count, width = tokens.shape
    _, part, kinds, hidden = expert_weights.shape
    blocks = width // part
    vmem = pl.BlockSpec(memory_space=pltpu.VMEM)
    anywhere = pl.BlockSpec(memory_space=pl.ANY)
    pairs = pltpu.VMEM((SLOTS, 2, CAP, width), BF16)
    sem = pltpu.SemaphoreType.DMA
    shapes = (
        jax.ShapeDtypeStruct((count, width), BF16),
        jax.ShapeDtypeStruct((count, width), BF16),
        jax.ShapeDtypeStruct((kinds, part, hidden), BF16),
    )
    results = pl.pallas_call(
        kernel,
        out_shape=tuple(pltpu.VMEM(a.shape, a.dtype) for a in shapes),
        in_specs=[anywhere, vmem, vmem, anywhere, anywhere],
        out_specs=(vmem,) * 3,
        scratch_shapes=[
            pltpu.VMEM((blocks, kinds, part, hidden), BF16),
            pltpu.VMEM((blocks, kinds, part, hidden), BF16),
            pltpu.VMEM((2, 30, kinds, part // 4, hidden), BF16),
            *([pairs] * 4),
            *([pltpu.VMEM((ROWS, width), BF16)] * 2),
            *([pltpu.VMEM((ROWS, hidden), BF16)] * 3),
            *([pltpu.VMEM((ROWS, count), BF16)] * 2),
            *([pltpu.VMEM((count, width), BF16)] * 2),
            *([pltpu.VMEM((count, width), F32)] * 2),
            *(pltpu.VMEM((2, count, CAP * (hi - lo)), BF16) for lo, hi in CHUNKS),
            *([sem((SLOTS,))] * 4),
            sem((2, 20)), sem((2, 20)), sem((2, 30)), sem((2, 30)), sem((3,)),
        ],
        compiler_params=pltpu.CompilerParams(
            collective_id=0, has_side_effects=True, vmem_limit_bytes=57 * 1024 * 1024
        ),
        name="experts",
    )(tokens, expert_ids.T, gate_units.T, jnp.transpose(expert_weights[0], (1, 0, 2)), out_grad)
    moe_out, token_grad, weight_grad = pl.pallas_call(
        hand_out,
        out_shape=shapes,
        in_specs=[anywhere] * 3,
        out_specs=(anywhere,) * 3,
        scratch_shapes=[sem((3, 2))],
        name="hand_out",
    )(*(pltpu.with_memory_space_constraint(a, pltpu.VMEM) for a in results))
    return moe_out, token_grad, jnp.transpose(weight_grad, (1, 0, 2))[None]


def solution(mesh):
    rows = P(("dp", "fsdp", "expert"), None)
    split = P("expert", ("dp", "fsdp"), None, None)
    return jax.shard_map(
        on_device,
        mesh=mesh,
        in_specs=(rows, rows, rows, split, rows),
        out_specs=(rows, rows, split),
        check_vma=False,
    )
```

```python
import functools

import jax
import jax.numpy as jnp
from jax import lax
from jax.experimental import pallas as pl
from jax.experimental.pallas import tpu as pltpu
from jax.sharding import PartitionSpec as P

CAP = 24
SLOTS = 16
ROWS = CAP * SLOTS
MESH = pl.DeviceIdType.MESH
BF16 = jnp.bfloat16
F32 = jnp.float32

STEPS = (0, 7, 1, 6, 2, 5, 3, 4)
OFFSETS = [(dz, dc) for dz in STEPS for dc in (0, 1)]
OWN = OFFSETS.index((0, 0))
CHUNKS = ((0, 10), (10, 14), (14, 16))
PIECES = ((2, 4), (4, 6), (6, 10), (10, 14), (14, 16), (0, 2))


def place():
    dp, fsdp, expert = (lax.axis_index(n) for n in ("dp", "fsdp", "expert"))
    return lax.div(fsdp, 2), dp * 2 + lax.rem(fsdp, 2), lax.div(expert, 2), lax.rem(expert, 2)


def device(x, y, z, core):
    return (lax.div(y, 2), x * 2 + lax.rem(y, 2), z * 2 + core)


def others(lo, hi):
    return [slot for slot in range(lo, hi) if slot != OWN]


def kernel(
    tokens_in, ids, units, weights, out_grad_in,
    moe_out, token_grad, weight_grad,
    full, term, reduced, pair_send, pair_recv, ret_send, ret_recv, rows, grads, act, gate_grad, up_grad,
    pick, weigh, tokens, out_grad, moe_sum, grad_sum, spread_a, spread_b, spread_c,
    out_s, out_r, ret_s, ret_r, ag_s, ag_r, rs_s, rs_r, in_s,
):
    x, y, z, core = place()
    (row_send, grad_send), (row_recv, grad_recv), (res_send, back_send), (res_recv, back_recv) = (
        (ref.at[:, 0], ref.at[:, 1]) for ref in (pair_send, pair_recv, ret_send, ret_recv)
    )
    width = tokens.shape[1]
    hidden = weights.shape[2]
    token_count = tokens.shape[0]

    def peer(slot, sign):
        dz, dc = OFFSETS[slot]
        return device(x, y, lax.rem(z + (sign * dz) % 8, 8), lax.rem(core + dc, 2))

    def near(axis, step):
        if axis == 0:
            return device(lax.rem(x + step % 4, 4), y, z, core)
        return device(x, lax.rem(y + step % 4, 4), z, core)

    def block(half, first, second):
        dx, dy = (first, second) if half == 0 else (second, first)
        bx, by = lax.rem(x + dx % 4, 4), lax.rem(y + dy % 4, 4)
        return lax.div(by, 2) * 8 + bx * 2 + lax.rem(by, 2)

    barrier = pltpu.get_barrier_semaphore()
    for slot in others(0, SLOTS):
        pl.semaphore_signal(barrier, inc=1, device_id=peer(slot, 1), device_id_type=MESH)
    for axis in (0, 1):
        for step in (1, -1):
            pl.semaphore_signal(barrier, inc=1, device_id=near(axis, step), device_id_type=MESH)

    mine = block(0, 0, 0)
    loads = [
        pltpu.make_async_copy(src, dst, in_s.at[i])
        for i, (src, dst) in enumerate(
            ((tokens_in, tokens), (weights, full.at[mine]), (out_grad_in, out_grad))
        )
    ]
    for load in loads:
        load.start()

    shape = (ROWS, token_count)
    row = lax.broadcasted_iota(jnp.int32, shape, 0)
    slot_of = (row * 2731) >> 16
    rank_of = (row - slot_of * CAP).astype(F32)
    pair = slot_of >> 1
    dz = jnp.zeros(shape, jnp.int32)
    for k, step in enumerate(STEPS):
        dz = jnp.where(pair == k, step, dz)
    named = ((z + dz) & 7) * 2 + ((core + slot_of) & 1)
    chosen = jnp.zeros(shape, F32)
    for k in range(ids.shape[0]):
        chosen = chosen + jnp.where(
            ids[k : k + 1, :] == named, units[k : k + 1, :].astype(F32), 0.0
        )
    earlier = (
        lax.broadcasted_iota(jnp.int32, (token_count, token_count), 0)
        < lax.broadcasted_iota(jnp.int32, (token_count, token_count), 1)
    ).astype(F32).astype(BF16)
    ranking = jnp.dot(
        (chosen > 0.0).astype(F32).astype(BF16), earlier, preferred_element_type=F32
    )
    gate = jnp.where(ranking == rank_of, chosen, 0.0)
    weigh[...] = (gate * (1.0 / 256.0)).astype(BF16)
    pick[...] = (gate > 0.0).astype(F32).astype(BF16)

    sent = []

    def send(src, dst, send_sem, recv_sem, to):
        copy = pltpu.make_async_remote_copy(
            src_ref=src, dst_ref=dst, send_sem=send_sem, recv_sem=recv_sem,
            device_id=to, device_id_type=MESH,
        )
        copy.start()
        sent.append(copy)
        return copy

    ag = {}

    def part(which, half):
        base = 64 * half
        return {"w": pl.ds(base, 64), "p": pl.ds(base, 32), "q": pl.ds(base + 32, 32)}[which]

    def gather_send(half, index, at, which, axis, step):
        ref = full.at[at, :, part(which, half), :]
        ag[half, index] = send(ref, ref, ag_s.at[half, index], ag_r.at[half, index], near(axis, step))

    ITEMS = (0, -1, 1, 2)

    def gather_own(half):
        a1, a2 = (0, 1) if half == 0 else (1, 0)
        gather_send(half, 0, mine, "w", a1, 1)
        gather_send(half, 1, mine, "w", a1, -1)

    def gather_item(half, k):
        a2 = 1 if half == 0 else 0
        at = block(half, ITEMS[k], 0)
        gather_send(half, 4 + 4 * k, at, "w", a2, 1)
        gather_send(half, 5 + 4 * k, at, "w", a2, -1)

    def gather_forward_first(half):
        a1 = 0 if half == 0 else 1
        ag[half, 0].wait_recv()
        gather_send(half, 2, block(half, -1, 0), "p", a1, 1)
        ag[half, 1].wait_recv()
        gather_send(half, 3, block(half, 1, 0), "q", a1, -1)

    def gather_forward_item(half, k):
        a2 = 1 if half == 0 else 0
        ag[half, 4 + 4 * k].wait_recv()
        gather_send(half, 6 + 4 * k, block(half, ITEMS[k], -1), "p", a2, 1)
        ag[half, 5 + 4 * k].wait_recv()
        gather_send(half, 7 + 4 * k, block(half, ITEMS[k], 1), "q", a2, -1)

    out = {}
    routes = ((pick, tokens, row_send, row_recv), (weigh, out_grad, grad_send, grad_recv))

    def choose(piece, a):
        lo, hi = piece
        cols = 512
        table, source, src, _ = routes[a]
        if piece == PIECES[0]:
            loads[2 * a].wait()

        def tile(i, _):
            at = pl.ds(pl.multiple_of(i * cols, cols), cols)
            got = jnp.dot(
                table[CAP * lo : CAP * hi, :], source[:, at], preferred_element_type=F32
            )
            src[lo:hi, :, at] = got.reshape(hi - lo, CAP, cols).astype(BF16)
            return 0

        lax.fori_loop(0, width // cols, tile, 0, unroll=piece == PIECES[0])

    def post(piece):
        lo, hi = piece
        for slot in others(lo, hi):
            out[slot] = send(
                pair_send.at[slot], pair_recv.at[slot], out_s.at[slot], out_r.at[slot], peer(slot, 1)
            )
        if lo <= OWN < hi:
            pair_recv[OWN] = pair_send[OWN]

    choose(PIECES[0], 0)
    choose(PIECES[0], 1)
    pl.semaphore_wait(barrier, SLOTS - 1 + 4)
    post(PIECES[0])
    loads[1].wait()
    for half in (0, 1):
        gather_own(half)
    for half in (0, 1):
        gather_item(half, 0)
    for piece in PIECES[1:]:
        choose(piece, 0)
        choose(piece, 1)
        post(piece)
    spread = (spread_a, spread_b, spread_c)
    for (lo, hi), to in zip(CHUNKS, spread):
        for a, table in enumerate((weigh, pick)):
            to[a] = jnp.transpose(table[CAP * lo : CAP * hi, :].astype(F32)).astype(BF16)
    for half in (0, 1):
        gather_forward_first(half)
    for half in (0, 1):
        gather_item(half, 1)
        gather_item(half, 2)
    for half in (0, 1):
        gather_forward_item(half, 0)
    for half in (0, 1):
        ag[half, 2].wait_recv()
        ag[half, 3].wait_recv()
        gather_item(half, 3)
    for k in (1, 2, 3):
        for half in (0, 1):
            gather_forward_item(half, k)
    for k in range(4):
        for half in (0, 1):
            ag[half, 6 + 4 * k].wait_recv()
            ag[half, 7 + 4 * k].wait_recv()

    ret = {}
    nt = (((1,), (1,)), ((), ()))
    tn = (((0,), (0,)), ((), ()))

    def experts(lo, hi):
        r0, r1 = CAP * lo, CAP * hi
        for slot in others(lo, hi):
            out[slot].wait_recv()

        def pack(i, _):
            at = pl.ds(pl.multiple_of(i * 512, 512), 512)
            for src, dst in ((row_recv, rows), (grad_recv, grads)):
                dst[r0:r1, at] = src[lo:hi, :, at].astype(F32).reshape(r1 - r0, 512).astype(BF16)
            return 0

        lax.fori_loop(0, width // 512, pack, 0)

        def inner(i, _):
            at = pl.ds(pl.multiple_of(i * 256, 256), 256)
            w = [full[:, j, :, at].reshape(width, 256) for j in range(3)]
            g = jnp.dot(rows[r0:r1, :], w[0], preferred_element_type=F32)
            u = jnp.dot(rows[r0:r1, :], w[1], preferred_element_type=F32)
            hg = jnp.dot(grads[r0:r1, :], w[2], preferred_element_type=F32)
            s = jax.nn.sigmoid(g)
            swish = g * s
            act[r0:r1, at] = (swish * u).astype(BF16)
            gate_grad[r0:r1, at] = (hg * u * s * (1.0 + g * (1.0 - s))).astype(BF16)
            up_grad[r0:r1, at] = (hg * swish).astype(BF16)
            return 0

        lax.fori_loop(0, hidden // 256, inner, 0)

        def outer(i, _):
            at = pl.ds(pl.multiple_of(i * 256, 256), 256)
            w = [full[pl.ds(2 * i, 2), j].reshape(256, hidden) for j in range(3)]
            res = lax.dot_general(act[r0:r1, :], w[2], nt, preferred_element_type=F32)
            res_send[lo:hi, :, at] = res.reshape(hi - lo, CAP, 256).astype(BF16)
            back = lax.dot_general(gate_grad[r0:r1, :], w[0], nt, preferred_element_type=F32)
            back = back + lax.dot_general(up_grad[r0:r1, :], w[1], nt, preferred_element_type=F32)
            back_send[lo:hi, :, at] = back.reshape(hi - lo, CAP, 256).astype(BF16)
            return 0

        lax.fori_loop(0, width // 256, outer, 0)
        for slot in others(lo, hi):
            ret[slot] = send(
                ret_send.at[slot], ret_recv.at[slot], ret_s.at[slot], ret_r.at[slot], peer(slot, -1)
            )
        if lo <= OWN < hi:
            ret_recv[OWN] = ret_send[OWN]

    for lo, hi in CHUNKS:
        experts(lo, hi)

    def terms(i, _):
        at = pl.ds(pl.multiple_of(i * 256, 256), 256)
        for j, (left, right) in enumerate(((rows, gate_grad), (rows, up_grad), (grads, act))):
            got = lax.dot_general(left[:, at], right[...], tn, preferred_element_type=F32)
            term[pl.ds(2 * i, 2), j] = got.reshape(2, 128, hidden).astype(BF16)
        return 0

    lax.fori_loop(0, width // 256, terms, 0)

    rs = {}

    def reduce_send(half, index, at, which, axis, step):
        rs[half, index] = send(
            term.at[at, :, part(which, half), :], reduced.at[half, index],
            rs_s.at[half, index], rs_r.at[half, index], near(axis, step),
        )

    def add_into(half, at, which, indices):
        rows_at = part(which, half)
        for j in range(3):
            total = term[at, j, rows_at, :].astype(F32)
            for index in indices:
                total = total + reduced[half, index, j].astype(F32)
            term[at, j, rows_at, :] = total.astype(BF16)

    def ring(half, base, axis, at):
        def start():
            reduce_send(half, base + 0, at(2), "q", axis, 1)
            reduce_send(half, base + 1, at(2), "p", axis, -1)
            reduce_send(half, base + 2, at(1), "p", axis, 1)
            reduce_send(half, base + 3, at(-1), "q", axis, -1)

        def forward():
            rs[half, base + 0].wait_recv()
            add_into(half, at(1), "q", (base + 0,))
            reduce_send(half, base + 4, at(1), "q", axis, 1)
            rs[half, base + 1].wait_recv()
            add_into(half, at(-1), "p", (base + 1,))
            reduce_send(half, base + 5, at(-1), "p", axis, -1)

        def finish():
            for index in (2, 5):
                rs[half, base + index].wait_recv()
            add_into(half, at(0), "p", (base + 2, base + 5))
            for index in (3, 4):
                rs[half, base + index].wait_recv()
            add_into(half, at(0), "q", (base + 3, base + 4))

        return start, forward, finish

    first = {}
    ORDER = (2, 1, -1, 0)
    for k, i in enumerate(ORDER):
        for half in (0, 1):
            first[half, k] = ring(
                half, 6 * k, 1 if half == 0 else 0, functools.partial(block, half, i)
            )
    second = {
        half: ring(half, 24, 0 if half == 0 else 1, lambda j, half=half: block(half, j, 0))
        for half in (0, 1)
    }
    tables = ((res_recv, moe_sum, moe_out), (back_recv, grad_sum, token_grad))

    def combine(n, a):
        lo, hi = CHUNKS[n]
        source, total, result = tables[a]
        if a == 0:
            for slot in others(lo, hi):
                ret[slot].wait_recv()

        def tile(i, _):
            at = pl.ds(pl.multiple_of(i * 512, 512), 512)
            got = source[lo:hi, :, at].astype(F32).reshape(CAP * (hi - lo), 512).astype(BF16)
            value = jnp.dot(spread[n][a], got, preferred_element_type=F32)
            if n > 0:
                value = total[:, at] + value
            if hi < SLOTS:
                total[:, at] = value
            else:
                result[:, at] = value.astype(BF16)
            return 0

        lax.fori_loop(0, width // 512, tile, 0, unroll=hi == SLOTS)

    for stage in (0, 1):
        for k in range(4):
            for half in (0, 1):
                first[half, k][stage]()
    for a in (0, 1):
        combine(0, a)
    for k in range(4):
        for half in (0, 1):
            first[half, k][2]()
    for stage in (0, 1, 2):
        for half in (0, 1):
            second[half][stage]()
    weight_grad[...] = term[mine]
    for n in (1, 2):
        for a in (0, 1):
            combine(n, a)
    for copy in sent:
        copy.wait_send()


def hand_out(*refs):
    sources, targets, sems = refs[:3], refs[3:6], refs[6]
    copies = []
    for i, (src, dst) in enumerate(zip(sources, targets)):
        parts = 2 if src.shape[0] % 2 == 0 else 1
        size = src.shape[0] // parts
        for k in range(parts):
            at = pl.ds(k * size, size)
            copies.append(pltpu.make_async_copy(src.at[at], dst.at[at], sems.at[i, k]))
    for copy in copies:
        copy.start()
    for copy in copies:
        copy.wait()


def on_device(tokens, expert_ids, gate_units, expert_weights, out_grad):
    count, width = tokens.shape
    _, part, kinds, hidden = expert_weights.shape
    blocks = width // part
    vmem = pl.BlockSpec(memory_space=pltpu.VMEM)
    anywhere = pl.BlockSpec(memory_space=pl.ANY)
    pairs = pltpu.VMEM((SLOTS, 2, CAP, width), BF16)
    sem = pltpu.SemaphoreType.DMA
    shapes = (
        jax.ShapeDtypeStruct((count, width), BF16),
        jax.ShapeDtypeStruct((count, width), BF16),
        jax.ShapeDtypeStruct((kinds, part, hidden), BF16),
    )
    results = pl.pallas_call(
        kernel,
        out_shape=tuple(pltpu.VMEM(a.shape, a.dtype) for a in shapes),
        in_specs=[anywhere, vmem, vmem, anywhere, anywhere],
        out_specs=(vmem,) * 3,
        scratch_shapes=[
            pltpu.VMEM((blocks, kinds, part, hidden), BF16),
            pltpu.VMEM((blocks, kinds, part, hidden), BF16),
            pltpu.VMEM((2, 30, kinds, part // 4, hidden), BF16),
            *([pairs] * 4),
            *([pltpu.VMEM((ROWS, width), BF16)] * 2),
            *([pltpu.VMEM((ROWS, hidden), BF16)] * 3),
            *([pltpu.VMEM((ROWS, count), BF16)] * 2),
            *([pltpu.VMEM((count, width), BF16)] * 2),
            *([pltpu.VMEM((count, width), F32)] * 2),
            *(pltpu.VMEM((2, count, CAP * (hi - lo)), BF16) for lo, hi in CHUNKS),
            *([sem((SLOTS,))] * 4),
            sem((2, 20)), sem((2, 20)), sem((2, 30)), sem((2, 30)), sem((3,)),
        ],
        compiler_params=pltpu.CompilerParams(
            collective_id=0, has_side_effects=True, vmem_limit_bytes=57 * 1024 * 1024
        ),
        name="experts",
    )(tokens, expert_ids.T, gate_units.T, jnp.transpose(expert_weights[0], (1, 0, 2)), out_grad)
    moe_out, token_grad, weight_grad = pl.pallas_call(
        hand_out,
        out_shape=shapes,
        in_specs=[anywhere] * 3,
        out_specs=(anywhere,) * 3,
        scratch_shapes=[sem((3, 2))],
        name="hand_out",
    )(*(pltpu.with_memory_space_constraint(a, pltpu.VMEM) for a in results))
    return moe_out, token_grad, jnp.transpose(weight_grad, (1, 0, 2))[None]


def solution(mesh):
    rows = P(("dp", "fsdp", "expert"), None)
    split = P("expert", ("dp", "fsdp"), None, None)
    return jax.shard_map(
        on_device,
        mesh=mesh,
        in_specs=(rows, rows, rows, split, rows),
        out_specs=(rows, rows, split),
        check_vma=False,
    )
```

```python
import functools

import jax
import jax.numpy as jnp
from jax import lax
from jax.experimental import pallas as pl
from jax.experimental.pallas import tpu as pltpu
from jax.sharding import PartitionSpec as P

CAP = 24
SLOTS = 16
ROWS = CAP * SLOTS
MESH = pl.DeviceIdType.MESH
BF16 = jnp.bfloat16
F32 = jnp.float32

STEPS = (0, 7, 1, 6, 2, 4, 5, 3)
OFFSETS = [(dz, dc) for dz in STEPS for dc in (0, 1)]
OWN = OFFSETS.index((0, 0))
CHUNKS = ((0, 10), (10, 12), (12, 16))
PIECES = ((2, 4), (4, 6), (6, 10), (10, 12), (12, 16), (0, 2))


def place():
    dp, fsdp, expert = (lax.axis_index(n) for n in ("dp", "fsdp", "expert"))
    return lax.div(fsdp, 2), dp * 2 + lax.rem(fsdp, 2), lax.div(expert, 2), lax.rem(expert, 2)


def device(x, y, z, core):
    return (lax.div(y, 2), x * 2 + lax.rem(y, 2), z * 2 + core)


def others(lo, hi):
    return [slot for slot in range(lo, hi) if slot != OWN]


def kernel(
    tokens_in, ids, units, weights, out_grad_in,
    moe_out, token_grad, weight_grad,
    full, term, reduced, pair_send, pair_recv, ret_send, ret_recv, rows, grads, act, gate_grad, up_grad,
    pick, weigh, tokens, out_grad, moe_sum, grad_sum, spread_a, spread_b, spread_c,
    out_s, out_r, ret_s, ret_r, ag_s, ag_r, rs_s, rs_r, in_s,
):
    x, y, z, core = place()
    (row_send, grad_send), (row_recv, grad_recv), (res_send, back_send), (res_recv, back_recv) = (
        (ref.at[:, 0], ref.at[:, 1]) for ref in (pair_send, pair_recv, ret_send, ret_recv)
    )
    width = tokens.shape[1]
    hidden = weights.shape[2]
    token_count = tokens.shape[0]

    def peer(slot, sign):
        dz, dc = OFFSETS[slot]
        return device(x, y, lax.rem(z + (sign * dz) % 8, 8), lax.rem(core + dc, 2))

    def near(axis, step):
        if axis == 0:
            return device(lax.rem(x + step % 4, 4), y, z, core)
        return device(x, lax.rem(y + step % 4, 4), z, core)

    def block(half, first, second):
        dx, dy = (first, second) if half == 0 else (second, first)
        bx, by = lax.rem(x + dx % 4, 4), lax.rem(y + dy % 4, 4)
        return lax.div(by, 2) * 8 + bx * 2 + lax.rem(by, 2)

    barrier = pltpu.get_barrier_semaphore()
    for slot in others(0, SLOTS):
        pl.semaphore_signal(barrier, inc=1, device_id=peer(slot, 1), device_id_type=MESH)
    for axis in (0, 1):
        for step in (1, -1):
            pl.semaphore_signal(barrier, inc=1, device_id=near(axis, step), device_id_type=MESH)

    mine = block(0, 0, 0)
    loads = [
        pltpu.make_async_copy(src, dst, in_s.at[i])
        for i, (src, dst) in enumerate(
            ((tokens_in, tokens), (weights, full.at[mine]), (out_grad_in, out_grad))
        )
    ]
    for load in loads:
        load.start()

    shape = (ROWS, token_count)
    row = lax.broadcasted_iota(jnp.int32, shape, 0)
    slot_of = (row * 2731) >> 16
    rank_of = (row - slot_of * CAP).astype(F32)
    pair = slot_of >> 1
    dz = jnp.zeros(shape, jnp.int32)
    for k, step in enumerate(STEPS):
        dz = jnp.where(pair == k, step, dz)
    named = ((z + dz) & 7) * 2 + ((core + slot_of) & 1)
    chosen = jnp.zeros(shape, F32)
    for k in range(ids.shape[0]):
        chosen = chosen + jnp.where(
            ids[k : k + 1, :] == named, units[k : k + 1, :].astype(F32), 0.0
        )
    earlier = (
        lax.broadcasted_iota(jnp.int32, (token_count, token_count), 0)
        < lax.broadcasted_iota(jnp.int32, (token_count, token_count), 1)
    ).astype(F32).astype(BF16)
    ranking = jnp.dot(
        (chosen > 0.0).astype(F32).astype(BF16), earlier, preferred_element_type=F32
    )
    gate = jnp.where(ranking == rank_of, chosen, 0.0)
    weigh[...] = (gate * (1.0 / 256.0)).astype(BF16)
    pick[...] = (gate > 0.0).astype(F32).astype(BF16)

    sent = []

    def send(src, dst, send_sem, recv_sem, to):
        copy = pltpu.make_async_remote_copy(
            src_ref=src, dst_ref=dst, send_sem=send_sem, recv_sem=recv_sem,
            device_id=to, device_id_type=MESH,
        )
        copy.start()
        sent.append(copy)
        return copy

    ag = {}

    def part(which, half):
        base = 64 * half
        return {"w": pl.ds(base, 64), "p": pl.ds(base, 32), "q": pl.ds(base + 32, 32)}[which]

    def gather_send(half, index, at, which, axis, step):
        ref = full.at[at, :, part(which, half), :]
        ag[half, index] = send(ref, ref, ag_s.at[half, index], ag_r.at[half, index], near(axis, step))

    ITEMS = (0, -1, 1, 2)

    def gather_own(half):
        a1, a2 = (0, 1) if half == 0 else (1, 0)
        gather_send(half, 0, mine, "w", a1, 1)
        gather_send(half, 1, mine, "w", a1, -1)

    def gather_item(half, k):
        a2 = 1 if half == 0 else 0
        at = block(half, ITEMS[k], 0)
        gather_send(half, 4 + 4 * k, at, "w", a2, 1)
        gather_send(half, 5 + 4 * k, at, "w", a2, -1)

    def gather_forward_first(half):
        a1 = 0 if half == 0 else 1
        ag[half, 0].wait_recv()
        gather_send(half, 2, block(half, -1, 0), "p", a1, 1)
        ag[half, 1].wait_recv()
        gather_send(half, 3, block(half, 1, 0), "q", a1, -1)

    def gather_forward_item(half, k):
        a2 = 1 if half == 0 else 0
        ag[half, 4 + 4 * k].wait_recv()
        gather_send(half, 6 + 4 * k, block(half, ITEMS[k], -1), "p", a2, 1)
        ag[half, 5 + 4 * k].wait_recv()
        gather_send(half, 7 + 4 * k, block(half, ITEMS[k], 1), "q", a2, -1)

    out = {}
    routes = ((pick, tokens, row_send, row_recv), (weigh, out_grad, grad_send, grad_recv))

    def choose(piece, a):
        lo, hi = piece
        cols = 512
        table, source, src, _ = routes[a]
        if piece == PIECES[0]:
            loads[2 * a].wait()

        def tile(i, _):
            at = pl.ds(pl.multiple_of(i * cols, cols), cols)
            got = jnp.dot(
                table[CAP * lo : CAP * hi, :], source[:, at], preferred_element_type=F32
            )
            src[lo:hi, :, at] = got.reshape(hi - lo, CAP, cols).astype(BF16)
            return 0

        lax.fori_loop(0, width // cols, tile, 0, unroll=piece == PIECES[0])

    def post(piece):
        lo, hi = piece
        for slot in others(lo, hi):
            out[slot] = send(
                pair_send.at[slot], pair_recv.at[slot], out_s.at[slot], out_r.at[slot], peer(slot, 1)
            )
        if lo <= OWN < hi:
            pair_recv[OWN] = pair_send[OWN]

    choose(PIECES[0], 0)
    choose(PIECES[0], 1)
    pl.semaphore_wait(barrier, SLOTS - 1 + 4)
    post(PIECES[0])
    loads[1].wait()
    for half in (0, 1):
        gather_own(half)
    for half in (0, 1):
        gather_item(half, 0)
    for piece in PIECES[1:]:
        choose(piece, 0)
        choose(piece, 1)
        post(piece)
    spread = (spread_a, spread_b, spread_c)
    for (lo, hi), to in zip(CHUNKS, spread):
        for a, table in enumerate((weigh, pick)):
            to[a] = jnp.transpose(table[CAP * lo : CAP * hi, :].astype(F32)).astype(BF16)
    for half in (0, 1):
        gather_forward_first(half)
    for half in (0, 1):
        gather_item(half, 1)
        gather_item(half, 2)
    for half in (0, 1):
        gather_forward_item(half, 0)
    for half in (0, 1):
        ag[half, 2].wait_recv()
        ag[half, 3].wait_recv()
        gather_item(half, 3)
    for k in (1, 2, 3):
        for half in (0, 1):
            gather_forward_item(half, k)
    for k in range(4):
        for half in (0, 1):
            ag[half, 6 + 4 * k].wait_recv()
            ag[half, 7 + 4 * k].wait_recv()

    ret = {}
    nt = (((1,), (1,)), ((), ()))
    tn = (((0,), (0,)), ((), ()))

    def experts(lo, hi):
        r0, r1 = CAP * lo, CAP * hi
        for slot in others(lo, hi):
            out[slot].wait_recv()

        def pack(i, _):
            at = pl.ds(pl.multiple_of(i * 512, 512), 512)
            for src, dst in ((row_recv, rows), (grad_recv, grads)):
                dst[r0:r1, at] = src[lo:hi, :, at].astype(F32).reshape(r1 - r0, 512).astype(BF16)
            return 0

        lax.fori_loop(0, width // 512, pack, 0)

        def inner(i, _):
            at = pl.ds(pl.multiple_of(i * 256, 256), 256)
            w = [full[:, j, :, at].reshape(width, 256) for j in range(3)]
            g = jnp.dot(rows[r0:r1, :], w[0], preferred_element_type=F32)
            u = jnp.dot(rows[r0:r1, :], w[1], preferred_element_type=F32)
            hg = jnp.dot(grads[r0:r1, :], w[2], preferred_element_type=F32)
            s = jax.nn.sigmoid(g)
            swish = g * s
            act[r0:r1, at] = (swish * u).astype(BF16)
            gate_grad[r0:r1, at] = (hg * u * s * (1.0 + g * (1.0 - s))).astype(BF16)
            up_grad[r0:r1, at] = (hg * swish).astype(BF16)
            return 0

        lax.fori_loop(0, hidden // 256, inner, 0)

        def outer(i, _):
            at = pl.ds(pl.multiple_of(i * 256, 256), 256)
            w = [full[pl.ds(2 * i, 2), j].reshape(256, hidden) for j in range(3)]
            res = lax.dot_general(act[r0:r1, :], w[2], nt, preferred_element_type=F32)
            res_send[lo:hi, :, at] = res.reshape(hi - lo, CAP, 256).astype(BF16)
            back = lax.dot_general(gate_grad[r0:r1, :], w[0], nt, preferred_element_type=F32)
            back = back + lax.dot_general(up_grad[r0:r1, :], w[1], nt, preferred_element_type=F32)
            back_send[lo:hi, :, at] = back.reshape(hi - lo, CAP, 256).astype(BF16)
            return 0

        lax.fori_loop(0, width // 256, outer, 0)
        for slot in others(lo, hi):
            ret[slot] = send(
                ret_send.at[slot], ret_recv.at[slot], ret_s.at[slot], ret_r.at[slot], peer(slot, -1)
            )
        if lo <= OWN < hi:
            ret_recv[OWN] = ret_send[OWN]

    for lo, hi in CHUNKS:
        experts(lo, hi)

    def terms(i, _):
        at = pl.ds(pl.multiple_of(i * 256, 256), 256)
        for j, (left, right) in enumerate(((rows, gate_grad), (rows, up_grad), (grads, act))):
            got = lax.dot_general(left[:, at], right[...], tn, preferred_element_type=F32)
            term[pl.ds(2 * i, 2), j] = got.reshape(2, 128, hidden).astype(BF16)
        return 0

    lax.fori_loop(0, width // 256, terms, 0)

    rs = {}

    def reduce_send(half, index, at, which, axis, step):
        rs[half, index] = send(
            term.at[at, :, part(which, half), :], reduced.at[half, index],
            rs_s.at[half, index], rs_r.at[half, index], near(axis, step),
        )

    def add_into(half, at, which, indices):
        rows_at = part(which, half)
        for j in range(3):
            total = term[at, j, rows_at, :].astype(F32)
            for index in indices:
                total = total + reduced[half, index, j].astype(F32)
            term[at, j, rows_at, :] = total.astype(BF16)

    def ring(half, base, axis, at):
        def start():
            reduce_send(half, base + 0, at(2), "q", axis, 1)
            reduce_send(half, base + 1, at(2), "p", axis, -1)
            reduce_send(half, base + 2, at(1), "p", axis, 1)
            reduce_send(half, base + 3, at(-1), "q", axis, -1)

        def forward():
            rs[half, base + 0].wait_recv()
            add_into(half, at(1), "q", (base + 0,))
            reduce_send(half, base + 4, at(1), "q", axis, 1)
            rs[half, base + 1].wait_recv()
            add_into(half, at(-1), "p", (base + 1,))
            reduce_send(half, base + 5, at(-1), "p", axis, -1)

        def finish():
            for index in (2, 5):
                rs[half, base + index].wait_recv()
            add_into(half, at(0), "p", (base + 2, base + 5))
            for index in (3, 4):
                rs[half, base + index].wait_recv()
            add_into(half, at(0), "q", (base + 3, base + 4))

        return start, forward, finish

    first = {}
    ORDER = (2, 1, -1, 0)
    for k, i in enumerate(ORDER):
        for half in (0, 1):
            first[half, k] = ring(
                half, 6 * k, 1 if half == 0 else 0, functools.partial(block, half, i)
            )
    second = {
        half: ring(half, 24, 0 if half == 0 else 1, lambda j, half=half: block(half, j, 0))
        for half in (0, 1)
    }
    tables = ((res_recv, moe_sum, moe_out), (back_recv, grad_sum, token_grad))

    def combine(n, a):
        lo, hi = CHUNKS[n]
        source, total, result = tables[a]
        if a == 0:
            for slot in others(lo, hi):
                ret[slot].wait_recv()

        def tile(i, _):
            at = pl.ds(pl.multiple_of(i * 512, 512), 512)
            got = source[lo:hi, :, at].astype(F32).reshape(CAP * (hi - lo), 512).astype(BF16)
            value = jnp.dot(spread[n][a], got, preferred_element_type=F32)
            if n > 0:
                value = total[:, at] + value
            if hi < SLOTS:
                total[:, at] = value
            else:
                result[:, at] = value.astype(BF16)
            return 0

        lax.fori_loop(0, width // 512, tile, 0, unroll=hi == SLOTS)

    for stage in (0, 1):
        for k in range(4):
            for half in (0, 1):
                first[half, k][stage]()
    for a in (0, 1):
        combine(0, a)
    for k in range(4):
        for half in (0, 1):
            first[half, k][2]()
    for stage in (0, 1, 2):
        for half in (0, 1):
            second[half][stage]()
    weight_grad[...] = term[mine]
    for n in (1, 2):
        for a in (0, 1):
            combine(n, a)
    for copy in sent:
        copy.wait_send()


def hand_out(*refs):
    sources, targets, sems = refs[:3], refs[3:6], refs[6]
    copies = []
    for i, (src, dst) in enumerate(zip(sources, targets)):
        parts = 2 if src.shape[0] % 2 == 0 else 1
        size = src.shape[0] // parts
        for k in range(parts):
            at = pl.ds(k * size, size)
            copies.append(pltpu.make_async_copy(src.at[at], dst.at[at], sems.at[i, k]))
    for copy in copies:
        copy.start()
    for copy in copies:
        copy.wait()


def on_device(tokens, expert_ids, gate_units, expert_weights, out_grad):
    count, width = tokens.shape
    _, part, kinds, hidden = expert_weights.shape
    blocks = width // part
    vmem = pl.BlockSpec(memory_space=pltpu.VMEM)
    anywhere = pl.BlockSpec(memory_space=pl.ANY)
    pairs = pltpu.VMEM((SLOTS, 2, CAP, width), BF16)
    sem = pltpu.SemaphoreType.DMA
    shapes = (
        jax.ShapeDtypeStruct((count, width), BF16),
        jax.ShapeDtypeStruct((count, width), BF16),
        jax.ShapeDtypeStruct((kinds, part, hidden), BF16),
    )
    results = pl.pallas_call(
        kernel,
        out_shape=tuple(pltpu.VMEM(a.shape, a.dtype) for a in shapes),
        in_specs=[anywhere, vmem, vmem, anywhere, anywhere],
        out_specs=(vmem,) * 3,
        scratch_shapes=[
            pltpu.VMEM((blocks, kinds, part, hidden), BF16),
            pltpu.VMEM((blocks, kinds, part, hidden), BF16),
            pltpu.VMEM((2, 30, kinds, part // 4, hidden), BF16),
            *([pairs] * 4),
            *([pltpu.VMEM((ROWS, width), BF16)] * 2),
            *([pltpu.VMEM((ROWS, hidden), BF16)] * 3),
            *([pltpu.VMEM((ROWS, count), BF16)] * 2),
            *([pltpu.VMEM((count, width), BF16)] * 2),
            *([pltpu.VMEM((count, width), F32)] * 2),
            *(pltpu.VMEM((2, count, CAP * (hi - lo)), BF16) for lo, hi in CHUNKS),
            *([sem((SLOTS,))] * 4),
            sem((2, 20)), sem((2, 20)), sem((2, 30)), sem((2, 30)), sem((3,)),
        ],
        compiler_params=pltpu.CompilerParams(
            collective_id=0, has_side_effects=True, vmem_limit_bytes=57 * 1024 * 1024
        ),
        name="experts",
    )(tokens, expert_ids.T, gate_units.T, jnp.transpose(expert_weights[0], (1, 0, 2)), out_grad)
    moe_out, token_grad, weight_grad = pl.pallas_call(
        hand_out,
        out_shape=shapes,
        in_specs=[anywhere] * 3,
        out_specs=(anywhere,) * 3,
        scratch_shapes=[sem((3, 2))],
        name="hand_out",
    )(*(pltpu.with_memory_space_constraint(a, pltpu.VMEM) for a in results))
    return moe_out, token_grad, jnp.transpose(weight_grad, (1, 0, 2))[None]


def solution(mesh):
    rows = P(("dp", "fsdp", "expert"), None)
    split = P("expert", ("dp", "fsdp"), None, None)
    return jax.shard_map(
        on_device,
        mesh=mesh,
        in_specs=(rows, rows, rows, split, rows),
        out_specs=(rows, rows, split),
        check_vma=False,
    )
```
